32 devices in a mesh: parts: 2 (over x), leaf: 16 (over z, y, core).
Axes of the slice: x: 2, y: 2, z: 4, core: 2. Of those that a mesh axis runs over, the one named last changes fastest.
Arguments:
- inputs: bfloat16 [65536, 64], P(('parts', 'leaf')), parts along dimension 0, may hold values from -6 to 6
- geometry: float32 [4, 65536], P(None, ('parts', 'leaf')), parts along dimension 1, as said below
- leaf_basis: bfloat16 [512, 128, 64], P(('parts', 'leaf')), parts along dimension 0, may hold values from -0.5 to 0.5
- transfer: bfloat16 [512, 64, 64], P(('parts', 'leaf')), parts along dimension 0, may hold values from -0.25 to 0.25
- leaf_coupling: bfloat16 [512, 16, 64, 64], P(('parts', 'leaf')), parts along dimension 0, may hold values from -0.1875 to 0.1875
- top_coupling: bfloat16 [64, 8, 64, 64], P(('parts', 'leaf')), parts along dimension 0, may hold values from -0.25 to 0.25
- near_list: int32 [512, 24], P(('parts', 'leaf')), parts along dimension 0, may hold values from -16 to 271, as said below
- recv_slot: int32 [512, 16], P(('parts', 'leaf')), parts along dimension 0, may hold values from 0 to 383, as said below
- send_leaf: int32 [32, 16, 24], P(('parts', 'leaf')), parts along dimension 0, may hold values from 0 to 15, as said below
- top_source: int32 [64, 8], P(('parts', 'leaf')), parts along dimension 0, may hold values from 0 to 31
Outputs:
- result_field: float32 [65536, 64], P(('parts', 'leaf')), parts along dimension 0
The draws below stay inside these ranges and needn't reach their ends.
There are 2 independent parts, one for each index of `parts`. The reference program is written for one: setup_inputs(seed, part) draws one part's arguments, and reference() takes and returns one part's arrays. A program takes and returns all parts, laid end to end along the dimension named above; each array names one. Nothing has to cross between parts.
Inputs may be any that keep to these rules, and one draw needn't show every extreme that they name: `geometry`: point q of leaf l = q // 128 has row 0 in [l / 16, l / 16 + 1), rows 1 and 2 in [0, 1), row 3 in [0.1, 1]. `near_list`: each leaf's 24 partners are distinct leaves within 16 of it, always including itself and the leaves 16 below and above it. `recv_slot`: within one block of 16 leaves the values are distinct: each of the 384 received slots is read by at most one far interaction. `send_leaf`: slots that no interaction reads hold 0.
All inputs are finite; a program needn't handle non-finite values.
Results may differ from the reference program's by a relative error of at most 0.003.
Values may be sent and summed in bfloat16 or wider, within the bound.
No kernel may reach another device: no remote copies, remote signals or barrier semaphores. Data moves between devices by JAX's collectives and lax.ppermute only.
A program may use at most 128 MiB of HBM per device.

```python
import jax
import jax.numpy as jnp
from jax import lax

LEAF = 128
RANK = 64
RHS = 64
LEAVES_DEV = 16
BRANCH = 8
REACH = 16
K_NEAR = 24
K_FAR = 16
K_TOP = 8
LEAVES = 256
POINTS = 32768
PARENTS = 32
SLOTS = 24
N_LEAF = 16


def routing_tables(key):
    key_permutation, key_peer, key_shuffle, key_owner = jax.random.split(key, 4)
    slot_total = N_LEAF * SLOTS
    requests = LEAVES_DEV * K_FAR
    column = jnp.arange(slot_total, dtype=jnp.int32)
    scores = jax.random.randint(key_permutation, (N_LEAF, slot_total), 0, 2 ** 20, dtype=jnp.int32) * slot_total + column[None, :]
    full_peer = jax.random.randint(key_peer, (N_LEAF, 1), 0, N_LEAF, dtype=jnp.int32)
    forced = (column[None, :] // SLOTS == full_peer) | (column[None, :] == 0) | (column[None, :] == slot_total - 1)
    scores = jnp.where(forced, column[None, :] - slot_total, scores)
    chosen = jnp.argsort(scores, axis=1, stable=True)[:, :requests]
    request_ids = jnp.arange(requests, dtype=jnp.int32)
    mixing = jax.random.randint(key_shuffle, (N_LEAF, requests), 0, 2 ** 20, dtype=jnp.int32) * requests + request_ids[None, :]
    shuffle = jnp.argsort(mixing, axis=1, stable=True)
    placed = jnp.take_along_axis(chosen, shuffle, axis=1).astype(jnp.int32)
    owners = jax.random.randint(key_owner, (N_LEAF, requests), 0, LEAVES_DEV, dtype=jnp.int32)
    owners = owners.at[:, 0].set(0).at[:, 1].set(LEAVES_DEV - 1)
    device_rows = jnp.arange(N_LEAF, dtype=jnp.int32)[:, None]
    slot_table = jnp.zeros((N_LEAF, slot_total), jnp.int32).at[device_rows, placed].set(owners)
    return (placed.reshape(N_LEAF * LEAVES_DEV, K_FAR), slot_table.reshape(N_LEAF, N_LEAF, SLOTS).transpose(1, 0, 2))


def draw_recv_slot(key, part):
    return routing_tables(key)[0]


def draw_send_leaf(key, part):
    return routing_tables(key)[1]


def draw_near_list(key, part):
    key = jax.random.fold_in(key, 2)
    span_total = 2 * REACH + 1
    column = jnp.arange(span_total, dtype=jnp.int32)
    scores = jax.random.randint(key, (LEAVES, span_total), 0, 2 ** 20, dtype=jnp.int32) * span_total + column[None, :]
    forced = (column == 0) | (column == REACH) | (column == span_total - 1)
    scores = jnp.where(forced[None, :], column[None, :] - span_total, scores)
    picks = jnp.argsort(scores, axis=1, stable=True)[:, :K_NEAR].astype(jnp.int32)
    return (jnp.arange(LEAVES, dtype=jnp.int32)[:, None] + picks - REACH).astype(jnp.int32)


def draw_geometry(key, part):
    key = jax.random.fold_in(key, 1)
    key_place, key_matrix = jax.random.split(key, 2)
    place = jax.random.uniform(key_place, (3, POINTS), jnp.float32)
    leaf_ids = (jnp.arange(POINTS, dtype=jnp.int32) // LEAF).astype(jnp.float32)
    along = leaf_ids / REACH + place[0]
    weight_entries = jnp.exp(jax.random.uniform(key_matrix, (POINTS,), jnp.float32, jnp.log(0.1), 0.0))
    return jnp.stack([along, place[1], place[2], weight_entries]).astype(jnp.float32)


def with_ends(array, stream_key, low, top_value):
    spot = [jax.random.randint(jax.random.fold_in(stream_key, axis), (), 0, length) for axis, length in enumerate(array.shape)]
    main_axis = array.shape.index(max(array.shape))
    beside = spot[:main_axis] + [(spot[main_axis] + 1) % array.shape[main_axis]] + spot[main_axis + 1:]
    return array.at[tuple(spot)].set(low).at[tuple(beside)].set(top_value)


def levels(own_key, extent, cuts, least, largest):
    def one(axis_at, blocks):
        draws = jax.random.uniform(jax.random.fold_in(jax.random.fold_in(own_key, 6), axis_at), (blocks,), jnp.float32, least / len(cuts), largest / len(cuts))
        return jnp.repeat(jnp.exp(draws), extent[axis_at] // blocks).reshape((-1,) + (1,) * (len(extent) - axis_at - 1))

    factor_of = one(*cuts[0])
    for cut in cuts[1:]:
        factor_of = factor_of * one(*cut)
    return factor_of


def gaussian(rng, shape, spread, reach, cuts=(), kind=jnp.bfloat16):
    result = jax.random.normal(rng, shape, jnp.float32) * spread
    if len(cuts) > 0:
        result = levels(rng, shape, cuts, -0.22, 0.18) * result
    return jnp.clip(result, min=-reach, max=reach).astype(kind)


def setup_inputs(seed: int = 0, part: int = 0) -> dict:
    key_of = jax.random.split(jax.random.key(seed), 11)
    own_keys = jax.random.split(jax.random.fold_in(key_of[10], part), 11)
    return {
        "inputs": gaussian(own_keys[0], (POINTS, RHS), 1.0, 6.0, ((0, 16),)),
        "geometry": draw_geometry(jax.random.fold_in(jax.random.fold_in(key_of[10], part), 71), part),
        "leaf_basis": gaussian(own_keys[2], (LEAVES, LEAF, RANK), LEAF ** -0.5, 0.5, ((0, 16),)),
        "transfer": gaussian(own_keys[3], (LEAVES, RANK, RANK), (RANK * BRANCH) ** -0.5, 0.25, ((0, 16),)),
        "leaf_coupling": gaussian(own_keys[4], (LEAVES, K_FAR, RANK, RANK), (RANK * K_FAR) ** -0.5, 0.1875, ((0, 16),)),
        "top_coupling": gaussian(own_keys[5], (PARENTS, K_TOP, RANK, RANK), (RANK * K_TOP) ** -0.5, 0.25, ((0, 16),)),
        "near_list": draw_near_list(jax.random.fold_in(jax.random.fold_in(key_of[10], part), 71), part),
        "recv_slot": draw_recv_slot(jax.random.fold_in(jax.random.fold_in(key_of[10], part), 71), part),
        "send_leaf": draw_send_leaf(jax.random.fold_in(jax.random.fold_in(key_of[10], part), 71), part),
        "top_source": with_ends(jax.random.randint(own_keys[9], (PARENTS, K_TOP), 0, PARENTS), jax.random.fold_in(own_keys[9], 1), 0, PARENTS - 1).astype(jnp.int32),
    }


coulomb_scale = 0.07957747154594767
soften = 0.0025

def kernel_block(targets, sources):
    delta_x = targets[0][None, :, None] - sources[0][:, None, :]
    delta_y = targets[1][None, :, None] - sources[1][:, None, :]
    delta_z = targets[2][None, :, None] - sources[2][:, None, :]
    dist_sq = delta_x * delta_x + delta_y * delta_y + delta_z * delta_z
    return (sources[3][:, None, :] * (coulomb_scale * lax.rsqrt(dist_sq + soften))).astype(jnp.bfloat16)

def reference(inputs, geometry, leaf_basis, transfer, leaf_coupling, top_coupling, near_list, recv_slot, send_leaf, top_source):
    leaf_inputs = inputs.reshape(LEAVES, LEAF, RHS)
    basis_wide = leaf_basis.astype(jnp.float32)
    transfer_expanded = transfer.astype(jnp.float32)
    leaf_coef = jnp.einsum('lpr,lps->lrs', basis_wide, leaf_inputs.astype(jnp.float32)).astype(jnp.bfloat16)
    upper_coef = jnp.einsum('pcqr,pcqs->prs', transfer_expanded.reshape(PARENTS, BRANCH, RANK, RANK), leaf_coef.astype(jnp.float32).reshape(PARENTS, BRANCH, RANK, RHS)).astype(jnp.bfloat16)
    upper_field = jnp.einsum('pkab,pkbs->pas', top_coupling.astype(jnp.float32), upper_coef[top_source].astype(jnp.float32)).astype(jnp.bfloat16)
    target_dev = (jnp.arange(LEAVES, dtype=jnp.int32) // LEAVES_DEV)[:, None]
    source_dev = recv_slot // SLOTS
    owner_leaf = send_leaf[source_dev, target_dev, recv_slot % SLOTS]
    sources = source_dev * LEAVES_DEV + owner_leaf
    panels = leaf_coef[sources].astype(jnp.float32)
    leaf_potential = jnp.einsum('lkab,lkbs->las', leaf_coupling.astype(jnp.float32), panels)
    upper_representation = jnp.repeat(upper_field, BRANCH, axis=0).astype(jnp.float32)
    summed_potential = (leaf_potential + jnp.einsum('qjz,qzr->qjr', transfer_expanded, upper_representation)).astype(jnp.bfloat16)
    far_part = jnp.einsum('lpa,las->lps', basis_wide, summed_potential.astype(jnp.float32))
    leaf_points = geometry.reshape(4, LEAVES, LEAF)

    def near_leaf(item):
        near_ids, leaf_pos = item
        inside = ((near_ids >= 0) & (near_ids < LEAVES)).astype(jnp.float32)
        clipped = jnp.clip(near_ids, 0, LEAVES - 1).astype(jnp.int32)
        targets = leaf_points[:, leaf_pos]
        green_function = kernel_block(targets, leaf_points[:, clipped])
        partner_inputs = leaf_inputs[clipped].astype(jnp.float32) * inside[:, None, None]
        return jnp.einsum('kpq,kqs->ps', green_function.astype(jnp.float32), partner_inputs)
    near_part = lax.map(near_leaf, (near_list, jnp.arange(LEAVES, dtype=jnp.int32)))
    return (near_part + far_part).reshape(POINTS, RHS)
```

```python
import functools

import jax
import jax.numpy as jnp
from jax import lax
from jax.experimental import pallas as pl
from jax.experimental.pallas import tpu as pltpu
from jax.sharding import PartitionSpec as P

BRANCH = 8
REACH = 16
SCALE = 0.07957747154594767
SOFTEN = 0.0025
BF, F32 = jnp.bfloat16, jnp.float32
NN = (((1,), (0,)), ((), ()))
NT = (((1,), (1,)), ((), ()))
TN = (((0,), (0,)), ((), ()))
VMEM = pl.BlockSpec(memory_space=pltpu.VMEM)
SMEM = pl.BlockSpec(memory_space=pltpu.SMEM)
FEATS = 16


def dot(a, b, dims=NN):
    return lax.dot_general(a, b, dims, preferred_element_type=F32)


def params(mib):
    return pltpu.CompilerParams(vmem_limit_bytes=mib * 2**20)


def parts_of(x):
    high = x.astype(BF).astype(F32)
    mid = (x - high).astype(BF).astype(F32)
    low = (x - high - mid).astype(BF).astype(F32)
    return high, mid, low


def by_row(rows, values):
    which = lax.rem(rows, 5)
    out = jnp.zeros(rows.shape, F32)
    for j, value in enumerate(values):
        out = jnp.where(which == j, value, out)
    return jnp.where(rows < 15, out, 0.0)


def source_rows(rows, x, y, z, gain):
    wide = by_row(
        rows,
        (-2.0 * gain * x, -2.0 * gain * y, -2.0 * gain * z, gain, gain * (x * x + y * y + z * z + SOFTEN)),
    )
    high, mid, low = parts_of(wide)
    return jnp.where(rows < 5, high, jnp.where(rows < 10, mid, low)).astype(BF)


def pack_kernel(me_ref, in_ref, geo_ref, basis_ref, transfer_ref, send_ref, shard_ref, left_ref, right_ref, own_ref, target_ref):
    leaves, rank, leaf = basis_ref.shape
    rhs, points = in_ref.shape
    center = (me_ref[0] + 1).astype(F32)
    x = geo_ref[0:1, :] - center
    y = geo_ref[1:2, :] - 0.5
    z = geo_ref[2:3, :] - 0.5
    scaled = SCALE * geo_ref[3:4, :]
    gain = 1.0 / (scaled * scaled)
    rows = lax.broadcasted_iota(jnp.int32, (FEATS, points), 0)
    right_ref[rhs:, :] = source_rows(rows, x - 1.0, y, z, gain)
    left_ref[rhs:, :] = source_rows(rows, x + 1.0, y, z, gain)
    own_ref[rhs:, :] = source_rows(rows, x, y, z, gain)
    all_in = in_ref[...]
    right_ref[:rhs, :] = all_in
    left_ref[:rhs, :] = all_in
    own_ref[:rhs, :] = all_in
    high, mid, low = parts_of(by_row(rows, (x, y, z, x * x + y * y + z * z, jnp.ones_like(x))))
    target_ref[0:FEATS, :] = high.astype(BF)
    target_ref[FEATS : 2 * FEATS, :] = jnp.where(rows < 10, mid, 0.0).astype(BF)
    target_ref[2 * FEATS : 3 * FEATS, :] = jnp.where(rows < 5, low, 0.0).astype(BF)

    blank = jnp.zeros((rhs, leaf), BF)
    lanes = lax.broadcasted_iota(jnp.int32, (rank, 2 * rhs), 1)
    uppers = leaves // BRANCH
    upper = [jnp.zeros((rank, 2 * rhs), F32) for _ in range(uppers)]
    for pair in range(leaves // 2):
        a, b = 2 * pair, 2 * pair + 1
        xa = in_ref[:, a * leaf : (a + 1) * leaf]
        xb = in_ref[:, b * leaf : (b + 1) * leaf]
        weights = jnp.concatenate(
            [jnp.concatenate([xa, blank], axis=1), jnp.concatenate([blank, xb], axis=1)], axis=0
        )
        coef = dot(jnp.concatenate([basis_ref[a], basis_ref[b]], axis=1), weights, NT).astype(BF)
        shard_ref[pair * rank : (pair + 1) * rank, :] = coef
        both = jnp.concatenate(
            [jnp.where(lanes < rhs, coef, jnp.zeros_like(coef)), jnp.where(lanes < rhs, jnp.zeros_like(coef), coef)],
            axis=0,
        )
        moved = jnp.concatenate([transfer_ref[a], transfer_ref[b]], axis=0)
        upper[a // BRANCH] += dot(moved, both, TN)
    for p in range(0, uppers, 2):
        left = upper[p] + pltpu.roll(upper[p], rhs, 1)
        right = upper[p + 1] + pltpu.roll(upper[p + 1], rhs, 1)
        at = leaves // 2 * rank + p // 2 * rank
        shard_ref[at : at + rank, :] = jnp.where(lanes < rhs, left, right).astype(BF)
    at = (leaves + uppers) // 2 * rank
    shard_ref[at:, :] = jnp.zeros((shard_ref.shape[0] - at, 2 * rhs), BF)
    shard_ref[at : at + send_ref.shape[0], 0 : send_ref.shape[1]] = send_ref[...].astype(F32).astype(BF)


def near_kernel(count, me_ref, list_ref, own_ref, left_ref, right_ref, target_ref, out_ref, block_ref):
    wide, points = own_ref.shape
    rhs = out_ref.shape[0]
    leaves, near = list_ref.shape
    leaf = points // leaves
    for side, ref in enumerate((left_ref, own_ref, right_ref)):
        for j in range(leaves):
            block_ref[side * leaves + j] = ref[:, j * leaf : (j + 1) * leaf]

    def blank(side):
        rows = lax.broadcasted_iota(jnp.int32, (wide - rhs, leaf), 0)
        for j in range(leaves):
            block_ref[side * leaves + j, rhs:, :] = jnp.where(rows == 4, 1.0, 0.0).astype(BF)

    pl.when(me_ref[0] == 0)(lambda: blank(0))
    pl.when(me_ref[0] == count - 1)(lambda: blank(2))

    def one(l, carry):
        at = pl.ds(pl.multiple_of(l * leaf, leaf), leaf)
        targets = target_ref[:, at].T
        total = jnp.zeros((rhs, leaf), F32)
        for k in range(0, near, 2):
            a, b = list_ref[l, k], list_ref[l, k + 1]
            feats = jnp.concatenate([block_ref[a, rhs:, :], block_ref[b, rhs:, :]], axis=1)
            feats = jnp.concatenate([feats, feats, feats], axis=0)
            green = lax.rsqrt(dot(targets, feats)).astype(BF)
            values = jnp.concatenate([block_ref[a, 0:rhs, :], block_ref[b, 0:rhs, :]], axis=1)
            total = total + dot(values, green, NT)
        out_ref[:, at] = total
        return carry

    lax.fori_loop(0, leaves, one, 0)


def coupling_kernel(c_ref, out_ref):
    leaves, far, rank, _ = c_ref.shape

    def one(l, carry):
        for k in range(0, far, 2):
            out_ref[l, :, k * rank : (k + 2) * rank] = jnp.concatenate([c_ref[l, k], c_ref[l, k + 1]], axis=1)
        return carry

    lax.fori_loop(0, leaves, one, 0)


def far_kernel(count, slots, me_ref, recv_ref, top_ref, all_ref, coupling_ref, top_coupling_ref, transfer_ref, basis_ref, near_ref, out_ref, owner_vmem, owner_ref, sem):
    leaves, rank, leaf = basis_ref.shape
    rhs = out_ref.shape[0]
    far = recv_ref.shape[1]
    uppers, top = top_ref.shape
    me = me_ref[0]
    bits = count.bit_length() - 1

    def place(device):
        gap = lax.bitwise_xor(device, me)
        out = jnp.int32(0)
        for i in range(bits):
            out = out + ((gap >> (bits - 1 - i)) & 1) * (1 << i)
        return out

    table_at = (leaves + uppers) // 2 * rank
    table_rows = all_ref.shape[1] - table_at
    rows = lax.broadcasted_iota(jnp.int32, (table_rows, 2 * rhs), 0)

    for p in range(count):
        table = all_ref[p, table_at:, :].astype(F32)
        mine = jnp.sum(jnp.where(rows == me, table, 0.0), axis=0, keepdims=True)
        owner_vmem[p : p + 1, :] = mine.astype(jnp.int32)
    copy = pltpu.make_async_copy(owner_vmem, owner_ref, sem)
    copy.start()
    copy.wait()

    lanes = lax.broadcasted_iota(jnp.int32, (rank, 2 * rhs), 1)
    half_of = (lanes >= rhs).astype(jnp.int32)

    def panel(position, index, base):
        at = pl.multiple_of(base + (index // 2) * rank, rank)
        both = all_ref[position, pl.ds(at, rank), :]
        return jnp.where(half_of == index % 2, both, jnp.zeros_like(both))

    for p in range(uppers):
        total = jnp.zeros((rank, 2 * rhs), F32)
        for k in range(top):
            source = top_ref[p, k]
            total = total + dot(top_coupling_ref[p, k], panel(place(source // uppers), source % uppers, leaves // 2 * rank))
        field = (total + pltpu.roll(total, rhs, 1)).astype(BF)

        def one(l, carry, field=field):
            total = jnp.zeros((rank, 2 * rhs), F32)
            for quad in range(far // 4):
                panels = []
                for k in range(4 * quad, 4 * quad + 4):
                    slot = recv_ref[l, k]
                    position = place(slot // slots)
                    panels.append(panel(position, owner_ref[position, slot % slots], 0))
                total = total + dot(
                    coupling_ref[l, :, 4 * quad * rank : 4 * (quad + 1) * rank], jnp.concatenate(panels, axis=0)
                )
            total = total + pltpu.roll(total, rhs, 1)
            total = (total + dot(transfer_ref[l], field)).astype(BF)
            at = pl.ds(pl.multiple_of(l * leaf, leaf), leaf)
            out_ref[:, at] = near_ref[:, at] + dot(total[:, 0:rhs], basis_ref[l], TN)
            return carry

        lax.fori_loop(p * BRANCH, (p + 1) * BRANCH, one, 0)


def body(count, inputs, geometry, leaf_basis, transfer, leaf_coupling, top_coupling, near_list, recv_slot, send_leaf, top_source):
    leaves, leaf, rank = leaf_basis.shape
    rhs = inputs.shape[1]
    points = leaves * leaf
    far = recv_slot.shape[1]
    slots = send_leaf.shape[2]
    uppers = leaves // BRANCH
    me = lax.axis_index("leaf").astype(jnp.int32)
    me_list = me.reshape(1)
    in_t = inputs.T
    basis_t = leaf_basis.transpose(0, 2, 1)
    table_rows = -(-count // 16) * 16
    shard_rows = (leaves + uppers) // 2 * rank + table_rows
    wide = jax.ShapeDtypeStruct((rhs + FEATS, points), BF)
    shard, to_left, to_right, own, targets = pl.pallas_call(
        pack_kernel,
        out_shape=(
            jax.ShapeDtypeStruct((shard_rows, 2 * rhs), BF),
            wide,
            wide,
            wide,
            jax.ShapeDtypeStruct((3 * FEATS, points), BF),
        ),
        in_specs=[SMEM] + [VMEM] * 5,
        out_specs=(VMEM,) * 5,
        compiler_params=params(32),
        name="pack",
    )(me_list, in_t, geometry, basis_t, transfer, send_leaf[0])

    up = [(i, i + 1) for i in range(count - 1)]
    down = [(i + 1, i) for i in range(count - 1)]
    left = lax.ppermute(to_right, "leaf", up)
    right = lax.ppermute(to_left, "leaf", down)

    everyone = shard[None]
    bit = count // 2
    while bit:
        other = lax.ppermute(everyone, "leaf", [(i, i ^ bit) for i in range(count)])
        everyone = jnp.concatenate([everyone, other], axis=0)
        bit //= 2

    local_ids = near_list - (me * leaves - REACH)
    near = pl.pallas_call(
        functools.partial(near_kernel, count),
        out_shape=jax.ShapeDtypeStruct((rhs, points), F32),
        in_specs=[SMEM] * 2 + [VMEM] * 4,
        out_specs=VMEM,
        scratch_shapes=[pltpu.VMEM((leaves + 2 * REACH, rhs + FEATS, leaf), BF)],
        compiler_params=params(32),
        name="near",
    )(me_list, local_ids, own, left, right, targets)

    coupling = pl.pallas_call(
        coupling_kernel,
        out_shape=jax.ShapeDtypeStruct((leaves, rank, far * rank), BF),
        in_specs=[VMEM],
        out_specs=VMEM,
        compiler_params=params(32),
        name="coupling",
    )(leaf_coupling)

    out = pl.pallas_call(
        functools.partial(far_kernel, count, slots),
        out_shape=jax.ShapeDtypeStruct((rhs, points), F32),
        in_specs=[SMEM] * 3 + [VMEM] * 6,
        out_specs=VMEM,
        scratch_shapes=[
            pltpu.VMEM((count, 2 * rhs), jnp.int32),
            pltpu.SMEM((count, 2 * rhs), jnp.int32),
            pltpu.SemaphoreType.DMA,
        ],
        compiler_params=params(40),
        name="far",
    )(me_list, recv_slot, top_source, everyone, coupling, top_coupling, transfer, basis_t, near)
    return out.T


def solution(mesh):
    spec = ("parts", "leaf")
    in_specs = (
        P(spec, None),
        P(None, spec),
        P(spec, None, None),
        P(spec, None, None),
        P(spec, None, None, None),
        P(spec, None, None, None),
        P(spec, None),
        P(spec, None),
        P(spec, None, None),
        P(spec, None),
    )
    step = functools.partial(body, mesh.shape["leaf"])
    return jax.shard_map(step, mesh=mesh, in_specs=in_specs, out_specs=P(spec, None), check_vma=False)
```

```python
import functools

import jax
import jax.numpy as jnp
from jax import lax
from jax.experimental import pallas as pl
from jax.experimental.pallas import tpu as pltpu
from jax.sharding import PartitionSpec as P

BRANCH = 8
REACH = 16
SCALE = 0.07957747154594767
SOFTEN = 0.0025
BF, F32 = jnp.bfloat16, jnp.float32
NN = (((1,), (0,)), ((), ()))
NT = (((1,), (1,)), ((), ()))
TN = (((0,), (0,)), ((), ()))
VMEM = pl.BlockSpec(memory_space=pltpu.VMEM)
SMEM = pl.BlockSpec(memory_space=pltpu.SMEM)
FEATS = 16


def dot(a, b, dims=NN):
    return lax.dot_general(a, b, dims, preferred_element_type=F32)


def params(mib):
    return pltpu.CompilerParams(vmem_limit_bytes=mib * 2**20)


def cost(us):
    return pl.CostEstimate(flops=int(us * 1e9), bytes_accessed=int(us * 1e6), transcendentals=0)


def parts_of(x):
    high = x.astype(BF).astype(F32)
    mid = (x - high).astype(BF).astype(F32)
    low = (x - high - mid).astype(BF).astype(F32)
    return high, mid, low


def by_row(rows, values):
    which = lax.rem(rows, 5)
    out = jnp.zeros(rows.shape, F32)
    for j, value in enumerate(values):
        out = jnp.where(which == j, value, out)
    return jnp.where(rows < 15, out, 0.0)


def source_rows(rows, x, y, z, gain):
    wide = by_row(
        rows,
        (-2.0 * gain * x, -2.0 * gain * y, -2.0 * gain * z, gain, gain * (x * x + y * y + z * z + SOFTEN)),
    )
    high, mid, low = parts_of(wide)
    return jnp.where(rows < 5, high, jnp.where(rows < 10, mid, low)).astype(BF)


def pack_kernel(me_ref, in_hbm, geo_hbm, basis_hbm, transfer_hbm, send_hbm, shard_ref, left_ref, right_ref, own_ref, target_ref, in_ref, geo_ref, basis_ref, transfer_ref, send_ref, sems):
    pairs = ((geo_hbm, geo_ref), (in_hbm, in_ref), (basis_hbm, basis_ref), (transfer_hbm, transfer_ref), (send_hbm, send_ref))
    copies = [pltpu.make_async_copy(src, dst, sems.at[i]) for i, (src, dst) in enumerate(pairs)]
    for copy in copies:
        copy.start()
    leaves, rank, leaf = basis_ref.shape
    rhs, points = in_ref.shape
    center = (me_ref[0] + 1).astype(F32)
    copies[0].wait()
    x = geo_ref[0:1, :] - center
    y = geo_ref[1:2, :] - 0.5
    z = geo_ref[2:3, :] - 0.5
    scaled = SCALE * geo_ref[3:4, :]
    gain = 1.0 / (scaled * scaled)
    rows = lax.broadcasted_iota(jnp.int32, (FEATS, points), 0)
    right_ref[rhs:, :] = source_rows(rows, x - 1.0, y, z, gain)
    left_ref[rhs:, :] = source_rows(rows, x + 1.0, y, z, gain)
    own_ref[rhs:, :] = source_rows(rows, x, y, z, gain)
    high, mid, low = parts_of(by_row(rows, (x, y, z, x * x + y * y + z * z, jnp.ones_like(x))))
    target_ref[0:FEATS, :] = high.astype(BF)
    target_ref[FEATS : 2 * FEATS, :] = jnp.where(rows < 10, mid, 0.0).astype(BF)
    target_ref[2 * FEATS : 3 * FEATS, :] = jnp.where(rows < 5, low, 0.0).astype(BF)
    copies[1].wait()
    all_in = in_ref[...]
    right_ref[:rhs, :] = all_in
    left_ref[:rhs, :] = all_in
    own_ref[:rhs, :] = all_in

    for copy in copies[2:]:
        copy.wait()
    blank = jnp.zeros((rhs, leaf), BF)
    lanes = lax.broadcasted_iota(jnp.int32, (rank, 2 * rhs), 1)
    uppers = leaves // BRANCH
    upper = [jnp.zeros((rank, 2 * rhs), F32) for _ in range(uppers)]
    for pair in range(leaves // 2):
        a, b = 2 * pair, 2 * pair + 1
        xa = in_ref[:, a * leaf : (a + 1) * leaf]
        xb = in_ref[:, b * leaf : (b + 1) * leaf]
        weights = jnp.concatenate(
            [jnp.concatenate([xa, blank], axis=1), jnp.concatenate([blank, xb], axis=1)], axis=0
        )
        coef = dot(jnp.concatenate([basis_ref[a], basis_ref[b]], axis=1), weights, NT).astype(BF)
        shard_ref[pair * rank : (pair + 1) * rank, :] = coef
        both = jnp.concatenate(
            [jnp.where(lanes < rhs, coef, jnp.zeros_like(coef)), jnp.where(lanes < rhs, jnp.zeros_like(coef), coef)],
            axis=0,
        )
        moved = jnp.concatenate([transfer_ref[a], transfer_ref[b]], axis=0)
        upper[a // BRANCH] += dot(moved, both, TN)
    for p in range(0, uppers, 2):
        left = upper[p] + pltpu.roll(upper[p], rhs, 1)
        right = upper[p + 1] + pltpu.roll(upper[p + 1], rhs, 1)
        at = leaves // 2 * rank + p // 2 * rank
        shard_ref[at : at + rank, :] = jnp.where(lanes < rhs, left, right).astype(BF)
    at = (leaves + uppers) // 2 * rank
    shard_ref[at:, :] = jnp.zeros((shard_ref.shape[0] - at, 2 * rhs), BF)
    shard_ref[at : at + send_ref.shape[0], 0 : send_ref.shape[1]] = send_ref[...].astype(F32).astype(BF)


def near_kernel(count, first, me_ref, list_ref, own_ref, left_ref, right_ref, target_ref, out_ref, block_ref):
    wide, points = own_ref.shape
    rhs, some = out_ref.shape
    leaves, near = list_ref.shape
    leaf = points // leaves
    me = me_ref[0]
    start = me * leaves - REACH
    for side, ref in enumerate((left_ref, own_ref, right_ref)):
        for j in range(leaves):
            block_ref[side * leaves + j] = ref[:, j * leaf : (j + 1) * leaf]

    def blank(side):
        rows = lax.broadcasted_iota(jnp.int32, (wide - rhs, leaf), 0)
        for j in range(leaves):
            block_ref[side * leaves + j, rhs:, :] = jnp.where(rows == 4, 1.0, 0.0).astype(BF)

    pl.when(me == 0)(lambda: blank(0))
    pl.when(me == count - 1)(lambda: blank(2))

    def one(l, carry):
        at = pl.ds(pl.multiple_of(l * leaf, leaf), leaf)
        targets = target_ref[:, pl.ds(pl.multiple_of((first + l) * leaf, leaf), leaf)].T
        total = jnp.zeros((rhs, leaf), F32)
        for k in range(0, near, 4):
            ids = [list_ref[first + l, k + i] - start for i in range(4)]
            feats = jnp.concatenate([block_ref[i, rhs:, :] for i in ids], axis=1)
            feats = jnp.concatenate([feats, feats, feats], axis=0)
            green = lax.rsqrt(dot(targets, feats)).astype(BF)
            values = jnp.concatenate([block_ref[i, 0:rhs, :] for i in ids], axis=1)
            total = total + dot(values, green, NT)
        out_ref[:, at] = total
        return carry

    lax.fori_loop(0, some // leaf, one, 0)


def coupling_kernel(c_ref, out_ref):
    leaves, far, rank, _ = c_ref.shape

    def one(l, carry):
        for k in range(0, far, 2):
            out_ref[l, :, k * rank : (k + 2) * rank] = jnp.concatenate([c_ref[l, k], c_ref[l, k + 1]], axis=1)
        return carry

    lax.fori_loop(0, leaves, one, 0)


def far_kernel(pieces, nears, me_ref, recv_ref, top_ref, *refs):
    piece_refs, refs = refs[:pieces], refs[pieces:]
    near_refs, refs = refs[:nears], refs[nears:]
    coupling_ref, top_coupling_ref, transfer_ref, basis_ref, out_ref, all_ref, owner_vmem, owner_ref, sem = refs
    leaves, rank, leaf = basis_ref.shape
    rhs = out_ref.shape[0]
    far = recv_ref.shape[1]
    uppers, top = top_ref.shape
    me = me_ref[0]
    table_at = (leaves + uppers) // 2 * rank
    table_rows = all_ref.shape[1] - table_at
    rows = lax.broadcasted_iota(jnp.int32, (table_rows, 2 * rhs), 0)
    depth = piece_refs[0].shape[0]
    for j, ref in enumerate(piece_refs):
        for i in range(depth):
            table = ref[i, table_at:, :].astype(F32)
            mine = jnp.sum(jnp.where(rows == me, table, 0.0), axis=0, keepdims=True)
            p = j * depth + i
            owner_vmem[p : p + 1, :] = mine.astype(jnp.int32)
    copy = pltpu.make_async_copy(owner_vmem, owner_ref, sem)
    copy.start()
    for j, ref in enumerate(piece_refs):
        all_ref[j * depth : (j + 1) * depth, :, :] = ref[...]

    lanes = lax.broadcasted_iota(jnp.int32, (rank, 2 * rhs), 1)
    half_of = (lanes >= rhs).astype(jnp.int32)

    def panel(position, index, base):
        at = pl.multiple_of(base + (index >> 1) * rank, rank)
        both = all_ref[position, pl.ds(at, rank), :]
        return jnp.where(half_of == (index & 1), both, jnp.zeros_like(both))

    fields = []
    for p in range(uppers):
        total = jnp.zeros((rank, 2 * rhs), F32)
        for k in range(top):
            word = top_ref[p, k]
            total = total + dot(top_coupling_ref[p, k], panel(word >> 8, word & 255, leaves // 2 * rank))
        fields.append((total + pltpu.roll(total, rhs, 1)).astype(BF))
    copy.wait()

    step = leaves // nears
    for part, near_ref in enumerate(near_refs):
        for j in range(step):
            l = part * step + j
            total = jnp.zeros((rank, 2 * rhs), F32)
            for quad in range(far // 4):
                panels = []
                for k in range(4 * quad, 4 * quad + 4):
                    word = recv_ref[l, k]
                    position = word >> 8
                    panels.append(panel(position, owner_ref[position, word & 255], 0))
                total = total + dot(
                    coupling_ref[l, :, 4 * quad * rank : 4 * (quad + 1) * rank], jnp.concatenate(panels, axis=0)
                )
            total = total + pltpu.roll(total, rhs, 1)
            total = (total + dot(transfer_ref[l], fields[l // BRANCH])).astype(BF)
            out_ref[:, l * leaf : (l + 1) * leaf] = near_ref[:, j * leaf : (j + 1) * leaf] + dot(
                total[:, 0:rhs], basis_ref[l], TN
            )


def body(count, inputs, geometry, leaf_basis, transfer, leaf_coupling, top_coupling, near_list, recv_slot, send_leaf, top_source):
    leaves, leaf, rank = leaf_basis.shape
    rhs = inputs.shape[1]
    points = leaves * leaf
    far = recv_slot.shape[1]
    slots = send_leaf.shape[2]
    uppers = leaves // BRANCH
    me = lax.axis_index("leaf").astype(jnp.int32)
    me_list = me.reshape(1)
    in_t = inputs.T
    basis_t = leaf_basis.transpose(0, 2, 1)
    table_rows = -(-count // 16) * 16
    shard_rows = (leaves + uppers) // 2 * rank + table_rows
    wide = jax.ShapeDtypeStruct((rhs + FEATS, points), BF)
    staged = (in_t, geometry, basis_t, transfer, send_leaf[0])
    shard, to_left, to_right, own, targets = pl.pallas_call(
        pack_kernel,
        out_shape=(
            jax.ShapeDtypeStruct((shard_rows, 2 * rhs), BF),
            wide,
            wide,
            wide,
            jax.ShapeDtypeStruct((3 * FEATS, points), BF),
        ),
        in_specs=[SMEM] + [pl.BlockSpec(memory_space=pltpu.HBM)] * 5,
        out_specs=(VMEM,) * 5,
        scratch_shapes=[pltpu.VMEM(a.shape, a.dtype) for a in staged] + [pltpu.SemaphoreType.DMA((5,))],
        compiler_params=params(32),
        cost_estimate=cost(2),
        name="pack",
    )(me_list, *staged)

    def swap(x, bit):
        return lax.ppermute(x, "leaf", [(i, i ^ bit) for i in range(count)])

    base = shard[None]
    high = count // 2
    while high > 8:
        base = jnp.concatenate([base, swap(base, high)], axis=0)
        high //= 2
    piece = {0: base}
    piece[8] = swap(base, 8)
    piece[4] = swap(base, 4)
    left = lax.ppermute(to_right, "leaf", [(i, i + 1) for i in range(count - 1)])
    right = lax.ppermute(to_left, "leaf", [(i + 1, i) for i in range(count - 1)])
    piece[2] = swap(base, 2)
    piece[12] = swap(piece[8], 4)
    piece[6] = swap(piece[4], 2)
    piece[10] = swap(piece[8], 2)
    piece[14] = swap(piece[12], 2)
    for j in (0, 2, 4, 8, 6, 10, 12, 14):
        piece[j + 1] = swap(piece[j], 1)

    def place(device):
        gap = lax.bitwise_xor(device, me)
        top = gap >> 4
        deep = jnp.zeros_like(gap)
        bits = (count // 16).bit_length() - 1
        for i in range(bits):
            deep = deep + ((top >> (bits - 1 - i)) & 1) * (1 << i)
        return (gap & 15) * (count // 16) + deep

    recv_words = place(recv_slot // slots) * 256 + recv_slot % slots
    top_words = place(top_source // uppers) * 256 + top_source % uppers

    coupling = pl.pallas_call(
        coupling_kernel,
        out_shape=jax.ShapeDtypeStruct((leaves, rank, far * rank), BF),
        in_specs=[VMEM],
        out_specs=VMEM,
        compiler_params=params(32),
        cost_estimate=cost(2),
        name="coupling",
    )(leaf_coupling)

    chunks = 4
    some = leaves // chunks
    nears = [
        pl.pallas_call(
            functools.partial(near_kernel, count, c * some),
            out_shape=jax.ShapeDtypeStruct((rhs, some * leaf), F32),
            in_specs=[SMEM] * 2 + [VMEM] * 4,
            out_specs=VMEM,
            scratch_shapes=[pltpu.VMEM((leaves + 2 * REACH, rhs + FEATS, leaf), BF)],
            compiler_params=params(32),
            cost_estimate=cost(4),
            name=f"near{c}",
        )(me_list, near_list, own, left, right, targets)
        for c in range(chunks)
    ]

    out = pl.pallas_call(
        functools.partial(far_kernel, 16, chunks),
        out_shape=jax.ShapeDtypeStruct((rhs, points), F32),
        in_specs=[SMEM] * 3 + [VMEM] * (16 + chunks + 4),
        out_specs=VMEM,
        scratch_shapes=[
            pltpu.VMEM((count, shard_rows, 2 * rhs), BF),
            pltpu.VMEM((count, 2 * rhs), jnp.int32),
            pltpu.SMEM((count, 2 * rhs), jnp.int32),
            pltpu.SemaphoreType.DMA,
        ],
        compiler_params=params(48),
        cost_estimate=cost(6),
        name="far",
    )(me_list, recv_words, top_words, *[piece[j] for j in range(16)], *nears, coupling, top_coupling, transfer, basis_t)
    return out.T


def solution(mesh):
    spec = ("parts", "leaf")
    in_specs = (
        P(spec, None),
        P(None, spec),
        P(spec, None, None),
        P(spec, None, None),
        P(spec, None, None, None),
        P(spec, None, None, None),
        P(spec, None),
        P(spec, None),
        P(spec, None, None),
        P(spec, None),
    )
    step = functools.partial(body, mesh.shape["leaf"])
    return jax.shard_map(step, mesh=mesh, in_specs=in_specs, out_specs=P(spec, None), check_vma=False)
```

```python
import functools

import jax
import jax.numpy as jnp
from jax import lax
from jax.experimental import pallas as pl
from jax.experimental.pallas import tpu as pltpu
from jax.sharding import PartitionSpec as P

BRANCH = 8
REACH = 16
SCALE = 0.07957747154594767
SOFTEN = 0.0025
BF, F32 = jnp.bfloat16, jnp.float32
NN = (((1,), (0,)), ((), ()))
NT = (((1,), (1,)), ((), ()))
TN = (((0,), (0,)), ((), ()))
VMEM = pl.BlockSpec(memory_space=pltpu.VMEM)
ANY = pl.BlockSpec(memory_space=pl.ANY)
SMEM = pl.BlockSpec(memory_space=pltpu.SMEM)
FEATS = 16


def dot(a, b, dims=NN):
    return lax.dot_general(a, b, dims, preferred_element_type=F32)


def params(mib):
    return pltpu.CompilerParams(vmem_limit_bytes=mib * 2**20)


def cost(us):
    return pl.CostEstimate(flops=int(us * 1e9), bytes_accessed=int(us * 1e6), transcendentals=0)


def parts_of(x):
    high = x.astype(BF).astype(F32)
    mid = (x - high).astype(BF).astype(F32)
    low = (x - high - mid).astype(BF).astype(F32)
    return high, mid, low


def by_row(rows, values):
    which = lax.rem(rows, 5)
    out = jnp.zeros(rows.shape, F32)
    for j, value in enumerate(values):
        out = jnp.where(which == j, value, out)
    return jnp.where(rows < 15, out, 0.0)


def source_rows(rows, x, y, z, gain):
    wide = by_row(
        rows,
        (-2.0 * gain * x, -2.0 * gain * y, -2.0 * gain * z, gain, gain * (x * x + y * y + z * z + SOFTEN)),
    )
    high, mid, low = parts_of(wide)
    return jnp.where(rows < 5, high, jnp.where(rows < 10, mid, low)).astype(BF)


def pack_kernel(me_ref, in_hbm, geo_hbm, basis_hbm, transfer_hbm, send_hbm, shard_ref, inner_ref, outer_ref, own_ref, target_ref, in_ref, geo_ref, basis_ref, transfer_ref, send_ref, sems):
    pairs = ((geo_hbm, geo_ref), (in_hbm, in_ref), (basis_hbm, basis_ref), (transfer_hbm, transfer_ref), (send_hbm, send_ref))
    copies = [pltpu.make_async_copy(src, dst, sems.at[i]) for i, (src, dst) in enumerate(pairs)]
    for copy in copies:
        copy.start()
    leaves, rank, leaf = basis_ref.shape
    rhs, points = in_ref.shape
    center = (me_ref[0] + 1).astype(F32)
    copies[0].wait()
    x = geo_ref[0:1, :] - center
    y = geo_ref[1:2, :] - 0.5
    z = geo_ref[2:3, :] - 0.5
    scaled = SCALE * geo_ref[3:4, :]
    gain = 1.0 / (scaled * scaled)
    rows = lax.broadcasted_iota(jnp.int32, (FEATS, points), 0)
    side = (1 - 2 * (me_ref[0] & 1)).astype(F32)
    inner_ref[rhs:, :] = source_rows(rows, x - side, y, z, gain)
    outer_ref[rhs:, :] = source_rows(rows, x + side, y, z, gain)
    own_ref[rhs:, :] = source_rows(rows, x, y, z, gain)
    high, mid, low = parts_of(by_row(rows, (x, y, z, x * x + y * y + z * z, jnp.ones_like(x))))
    target_ref[0:FEATS, :] = high.astype(BF)
    target_ref[FEATS : 2 * FEATS, :] = jnp.where(rows < 10, mid, 0.0).astype(BF)
    target_ref[2 * FEATS : 3 * FEATS, :] = jnp.where(rows < 5, low, 0.0).astype(BF)
    target_ref[3 * FEATS :, :] = jnp.zeros((FEATS, points), BF)
    copies[1].wait()
    all_in = in_ref[...]
    inner_ref[:rhs, :] = all_in
    outer_ref[:rhs, :] = all_in
    own_ref[:rhs, :] = all_in

    for copy in copies[2:]:
        copy.wait()
    blank = jnp.zeros((rhs, leaf), BF)
    lanes = lax.broadcasted_iota(jnp.int32, (rank, 2 * rhs), 1)
    uppers = leaves // BRANCH
    upper = [jnp.zeros((rank, 2 * rhs), F32) for _ in range(uppers)]
    for pair in range(leaves // 2):
        a, b = 2 * pair, 2 * pair + 1
        xa = in_ref[:, a * leaf : (a + 1) * leaf]
        xb = in_ref[:, b * leaf : (b + 1) * leaf]
        weights = jnp.concatenate(
            [jnp.concatenate([xa, blank], axis=1), jnp.concatenate([blank, xb], axis=1)], axis=0
        )
        coef = dot(jnp.concatenate([basis_ref[a], basis_ref[b]], axis=1), weights, NT).astype(BF)
        shard_ref[pair * rank : (pair + 1) * rank, :] = coef
        both = jnp.concatenate(
            [jnp.where(lanes < rhs, coef, jnp.zeros_like(coef)), jnp.where(lanes < rhs, jnp.zeros_like(coef), coef)],
            axis=0,
        )
        moved = jnp.concatenate([transfer_ref[a], transfer_ref[b]], axis=0)
        upper[a // BRANCH] += dot(moved, both, TN)
    for p in range(0, uppers, 2):
        left = upper[p] + pltpu.roll(upper[p], rhs, 1)
        right = upper[p + 1] + pltpu.roll(upper[p + 1], rhs, 1)
        at = leaves // 2 * rank + p // 2 * rank
        shard_ref[at : at + rank, :] = jnp.where(lanes < rhs, left, right).astype(BF)
    at = (leaves + uppers) // 2 * rank
    shard_ref[at:, :] = jnp.zeros((shard_ref.shape[0] - at, 2 * rhs), BF)
    shard_ref[at : at + send_ref.shape[0], 0 : send_ref.shape[1]] = send_ref[...].astype(F32).astype(BF)


def near_kernel(count, first, me_ref, list_ref, own_ref, inner_ref, outer_ref, target_ref, out_ref, block_ref):
    wide, points = own_ref.shape
    rhs, some = out_ref.shape
    leaves, near = list_ref.shape
    leaf = points // leaves
    me = me_ref[0]
    start = me * leaves - REACH
    odd = me & 1
    for base, ref in ((2 * (1 - odd) * leaves, inner_ref), (leaves, own_ref), (2 * odd * leaves, outer_ref)):
        for j in range(leaves):
            block_ref[base + j] = ref[:, j * leaf : (j + 1) * leaf]

    def blank(side):
        rows = lax.broadcasted_iota(jnp.int32, (wide - rhs, leaf), 0)
        for j in range(leaves):
            block_ref[side * leaves + j, rhs:, :] = jnp.where(rows == 4, 1.0, 0.0).astype(BF)

    pl.when(me == 0)(lambda: blank(0))
    pl.when(me == count - 1)(lambda: blank(2))

    lanes = lax.broadcasted_iota(jnp.int32, (leaf, 2 * rhs), 1)
    empty = jnp.zeros((4 * FEATS, leaf), BF)
    blank_tile = jnp.zeros((leaf, leaf), BF)
    for l in range(some // leaf):
        rows = target_ref[:, (first + l) * leaf : (first + l + 1) * leaf]
        low = jnp.concatenate([rows, empty], axis=0).T
        high = jnp.concatenate([empty, rows], axis=0).T
        targets = jnp.concatenate(
            [
                jnp.concatenate(two, axis=1)
                for two in ((low, blank_tile), (high, blank_tile), (blank_tile, low), (blank_tile, high))
            ],
            axis=0,
        )
        total = jnp.zeros((leaf, 2 * rhs), F32)
        for k in range(0, near, 8):
            ids = [list_ref[first + l, k + i] - start for i in range(8)]
            feats, values = [], []
            for a, b in zip(ids[0::2], ids[1::2], strict=True):
                feats += [jnp.concatenate([block_ref[a, rhs:, :], block_ref[b, rhs:, :]], axis=1)] * 4
                values.append(jnp.concatenate([block_ref[a, 0:rhs, :], block_ref[b, 0:rhs, :]], axis=1))
            green = lax.rsqrt(dot(targets, jnp.concatenate(feats, axis=0))).astype(BF)
            out = dot(green, jnp.concatenate(values, axis=0), NT)
            total = total + jnp.where(lanes < rhs, out[0:leaf, 0 : 2 * rhs], out[leaf : 2 * leaf, 0 : 2 * rhs])
            total = total + jnp.where(lanes < rhs, out[2 * leaf : 3 * leaf, 2 * rhs :], out[3 * leaf :, 2 * rhs :])
        turned = total.T
        out_ref[:, l * leaf : (l + 1) * leaf] = turned[0:rhs] + turned[rhs:]


def merge_kernel(a_ref, b_ref, out_ref):
    deep = a_ref.shape[0]
    out_ref[0:deep] = a_ref[...]
    out_ref[deep:] = b_ref[...]


def coupling_kernel(_, c_ref, top_ref, out_ref, top_out_ref):
    leaves, far, rank, _ = c_ref.shape
    uppers, top, _, _ = top_ref.shape
    for p in range(uppers):
        for k in range(0, top, 2):
            top_out_ref[p, :, k * rank : (k + 2) * rank] = jnp.concatenate([top_ref[p, k], top_ref[p, k + 1]], axis=1)

    def one(l, carry):
        for k in range(0, far, 2):
            out_ref[l, :, k * rank : (k + 2) * rank] = jnp.concatenate([c_ref[l, k], c_ref[l, k + 1]], axis=1)
        return carry

    lax.fori_loop(0, leaves, one, 0)


def far_kernel(pieces, nears, me_ref, recv_ref, top_ref, *refs):
    piece_refs, refs = refs[:pieces], refs[pieces:]
    near_refs, refs = refs[:nears], refs[nears:]
    coupling_ref, top_coupling_ref, transfer_ref, basis_ref, out_ref, all_ref, owner_vmem, owner_ref, sem = refs
    leaves, rank, leaf = basis_ref.shape
    rhs = out_ref.shape[0]
    far = recv_ref.shape[1]
    uppers, top = top_ref.shape
    me = me_ref[0]
    table_at = (leaves + uppers) // 2 * rank
    table_rows = all_ref.shape[1] - table_at
    rows = lax.broadcasted_iota(jnp.int32, (table_rows, 2 * rhs), 0)
    depth = piece_refs[0].shape[0]
    for j, ref in enumerate(piece_refs):
        for i in range(depth):
            table = ref[i, table_at:, :].astype(F32)
            mine = jnp.sum(jnp.where(rows == me, table, 0.0), axis=0, keepdims=True)
            p = j * depth + i
            owner_vmem[p : p + 1, :] = mine.astype(jnp.int32)
    copy = pltpu.make_async_copy(owner_vmem, owner_ref, sem)
    copy.start()
    for j, ref in enumerate(piece_refs):
        all_ref[j * depth : (j + 1) * depth, :, :] = ref[...]

    lanes = lax.broadcasted_iota(jnp.int32, (rank, 2 * rhs), 1)
    half_of = (lanes >= rhs).astype(jnp.int32)

    def panel(position, index, base):
        at = pl.multiple_of(base + (index >> 1) * rank, rank)
        both = all_ref[position, pl.ds(at, rank), :]
        return jnp.where(half_of == (index & 1), both, jnp.zeros_like(both))

    def sum_of(left, words, base):
        total = jnp.zeros((rank, 2 * rhs), F32)
        for quad in range(0, len(words), 4):
            panels = jnp.concatenate([panel(*word, base) for word in words[quad : quad + 4]], axis=0)
            total = total + dot(left[:, quad * rank : (quad + 4) * rank], panels)
        return total + pltpu.roll(total, rhs, 1)

    moved = []
    for p in range(uppers):
        words = [top_ref[p, k] for k in range(top)]
        field = sum_of(top_coupling_ref[p], [(word >> 8, word & 255) for word in words], leaves // 2 * rank).astype(BF)
        down = transfer_ref[p * BRANCH : (p + 1) * BRANCH].reshape(BRANCH * rank, rank)
        moved.append(dot(down, field))
    copy.wait()

    step = leaves // nears
    for l in range(0, leaves, 2):
        totals = []
        for i in (l, l + 1):
            words = [recv_ref[i, k] for k in range(far)]
            words = [(word >> 8, owner_ref[word >> 8, word & 255]) for word in words]
            at = i % BRANCH * rank
            totals.append(sum_of(coupling_ref[i], words, 0) + moved[i // BRANCH][at : at + rank])
        pair = jnp.where(lanes < rhs, totals[0], totals[1]).T.astype(BF)
        out = dot(pair, jnp.concatenate([basis_ref[l], basis_ref[l + 1]], axis=1))
        for i in range(2):
            j = (l + i) % step
            out_ref[:, (l + i) * leaf : (l + i + 1) * leaf] = (
                near_refs[l // step][:, j * leaf : (j + 1) * leaf]
                + out[i * rhs : (i + 1) * rhs, i * leaf : (i + 1) * leaf]
            )


def body(count, inputs, geometry, leaf_basis, transfer, leaf_coupling, top_coupling, near_list, recv_slot, send_leaf, top_source):
    leaves, leaf, rank = leaf_basis.shape
    rhs = inputs.shape[1]
    points = leaves * leaf
    far = recv_slot.shape[1]
    slots = send_leaf.shape[2]
    uppers = leaves // BRANCH
    me = lax.axis_index("leaf").astype(jnp.int32)
    me_list = me.reshape(1)
    in_t = inputs.T
    basis_t = leaf_basis.transpose(0, 2, 1)
    table_rows = -(-count // 16) * 16
    shard_rows = (leaves + uppers) // 2 * rank + table_rows
    wide = jax.ShapeDtypeStruct((rhs + FEATS, points), BF)
    staged = (in_t, geometry, basis_t, transfer, send_leaf[0])
    shard, to_inner, to_outer, own, targets = pl.pallas_call(
        pack_kernel,
        out_shape=(
            jax.ShapeDtypeStruct((shard_rows, 2 * rhs), BF),
            wide,
            wide,
            wide,
            jax.ShapeDtypeStruct((4 * FEATS, points), BF),
        ),
        in_specs=[SMEM] + [pl.BlockSpec(memory_space=pltpu.HBM)] * 5,
        out_specs=(VMEM,) * 5,
        scratch_shapes=[pltpu.VMEM(a.shape, a.dtype) for a in staged] + [pltpu.SemaphoreType.DMA((5,))],
        compiler_params=params(60),
        cost_estimate=cost(2),
        name="pack",
    )(me_list, *staged)

    def swap(x, bit):
        return lax.ppermute(x, "leaf", [(i, i ^ bit) for i in range(count)])

    base = shard[None]
    high = count // 2
    while high > 8:
        base = jnp.concatenate([base, swap(base, high)], axis=0)
        high //= 2
    deep = base.shape[0]
    far_side = swap(base, 8)
    inner = swap(to_inner, 1)
    outer = lax.ppermute(
        to_outer, "leaf", [pair for i in range(1, count - 1, 2) for pair in ((i, i + 1), (i + 1, i))]
    )
    both = pl.pallas_call(
        merge_kernel,
        out_shape=jax.ShapeDtypeStruct((2 * deep, *base.shape[1:]), BF),
        in_specs=[VMEM] * 2,
        out_specs=VMEM,
        compiler_params=params(32),
        cost_estimate=cost(1),
        name="merge",
    )(base, far_side)
    piece = {0: both}
    piece[4] = swap(both, 4)
    piece[2] = swap(both, 2)
    piece[6] = swap(piece[4], 2)
    for j in (0, 4, 2, 6):
        piece[j + 1] = swap(piece[j], 1)

    def place(device):
        gap = lax.bitwise_xor(device, me)
        top = gap >> 4
        out = (gap & 7) * (2 * deep) + ((gap >> 3) & 1) * deep
        bits = deep.bit_length() - 1
        for i in range(bits):
            out = out + ((top >> (bits - 1 - i)) & 1) * (1 << i)
        return out

    recv_words = place(recv_slot // slots) * 256 + recv_slot % slots
    top_words = place(top_source // uppers) * 256 + top_source % uppers

    coupling, top_wide = pl.pallas_call(
        coupling_kernel,
        out_shape=(
            jax.ShapeDtypeStruct((leaves, rank, far * rank), BF),
            jax.ShapeDtypeStruct((uppers, rank, top_source.shape[1] * rank), BF),
        ),
        in_specs=[ANY, VMEM, VMEM],
        out_specs=(VMEM,) * 2,
        compiler_params=params(32),
        cost_estimate=cost(2),
        name="coupling",
    )(both, leaf_coupling, top_coupling)

    chunks = 4
    some = leaves // chunks
    nears = [
        pl.pallas_call(
            functools.partial(near_kernel, count, c * some),
            out_shape=jax.ShapeDtypeStruct((rhs, some * leaf), F32),
            in_specs=[SMEM] * 2 + [VMEM] * 4,
            out_specs=VMEM,
            scratch_shapes=[pltpu.VMEM((leaves + 2 * REACH, rhs + FEATS, leaf), BF)],
            compiler_params=params(32),
            cost_estimate=cost(2.5),
            name=f"near{c}",
        )(me_list, near_list, own, inner, outer, targets)
        for c in range(chunks)
    ]

    out = pl.pallas_call(
        functools.partial(far_kernel, len(piece), chunks),
        out_shape=jax.ShapeDtypeStruct((rhs, points), F32),
        in_specs=[SMEM] * 3 + [VMEM] * (len(piece) + chunks + 4),
        out_specs=VMEM,
        scratch_shapes=[
            pltpu.VMEM((count, shard_rows, 2 * rhs), BF),
            pltpu.VMEM((count, 2 * rhs), jnp.int32),
            pltpu.SMEM((count, 2 * rhs), jnp.int32),
            pltpu.SemaphoreType.DMA,
        ],
        compiler_params=params(48),
        cost_estimate=cost(6),
        name="far",
    )(me_list, recv_words, top_words, *[piece[j] for j in range(len(piece))], *nears, coupling, top_wide, transfer, basis_t)
    return out.T


def solution(mesh):
    spec = ("parts", "leaf")
    in_specs = (
        P(spec, None),
        P(None, spec),
        P(spec, None, None),
        P(spec, None, None),
        P(spec, None, None, None),
        P(spec, None, None, None),
        P(spec, None),
        P(spec, None),
        P(spec, None, None),
        P(spec, None),
    )
    step = functools.partial(body, mesh.shape["leaf"])
    return jax.shard_map(step, mesh=mesh, in_specs=in_specs, out_specs=P(spec, None), check_vma=False)
```

```python
import functools

import jax
import jax.numpy as jnp
from jax import lax
from jax.experimental import pallas as pl
from jax.experimental.pallas import tpu as pltpu
from jax.sharding import PartitionSpec as P

BRANCH = 8
REACH = 16
SCALE = 0.07957747154594767
SOFTEN = 0.0025
BF, F32 = jnp.bfloat16, jnp.float32
NN = (((1,), (0,)), ((), ()))
NT = (((1,), (1,)), ((), ()))
TN = (((0,), (0,)), ((), ()))
VMEM = pl.BlockSpec(memory_space=pltpu.VMEM)
ANY = pl.BlockSpec(memory_space=pl.ANY)
SMEM = pl.BlockSpec(memory_space=pltpu.SMEM)
FEATS = 16


def dot(a, b, dims=NN):
    return lax.dot_general(a, b, dims, preferred_element_type=F32)


def params(mib):
    return pltpu.CompilerParams(vmem_limit_bytes=mib * 2**20)


def cost(us):
    return pl.CostEstimate(flops=int(us * 1e9), bytes_accessed=int(us * 1e6), transcendentals=0)


def parts_of(x):
    high = x.astype(BF).astype(F32)
    mid = (x - high).astype(BF).astype(F32)
    low = (x - high - mid).astype(BF).astype(F32)
    return high, mid, low


def by_row(rows, values):
    which = lax.rem(rows, 5)
    out = jnp.zeros(rows.shape, F32)
    for j, value in enumerate(values):
        out = jnp.where(which == j, value, out)
    return jnp.where(rows < 15, out, 0.0)


def source_rows(rows, x, y, z, gain):
    wide = by_row(
        rows,
        (-2.0 * gain * x, -2.0 * gain * y, -2.0 * gain * z, gain, gain * (x * x + y * y + z * z + SOFTEN)),
    )
    high, mid, low = parts_of(wide)
    return jnp.where(rows < 5, high, jnp.where(rows < 10, mid, low)).astype(BF)


def pack_kernel(me_ref, in_hbm, geo_hbm, basis_hbm, transfer_hbm, send_hbm, shard_ref, inner_ref, outer_ref, own_ref, target_ref, in_ref, geo_ref, basis_ref, transfer_ref, send_ref, sems):
    pairs = ((geo_hbm, geo_ref), (in_hbm, in_ref), (basis_hbm, basis_ref), (transfer_hbm, transfer_ref), (send_hbm, send_ref))
    copies = [pltpu.make_async_copy(src, dst, sems.at[i]) for i, (src, dst) in enumerate(pairs)]
    for copy in copies:
        copy.start()
    leaves, rank, leaf = basis_ref.shape
    rhs, points = in_ref.shape
    center = (me_ref[0] + 1).astype(F32)
    copies[0].wait()
    x = geo_ref[0:1, :] - center
    y = geo_ref[1:2, :] - 0.5
    z = geo_ref[2:3, :] - 0.5
    scaled = SCALE * geo_ref[3:4, :]
    gain = 1.0 / (scaled * scaled)
    rows = lax.broadcasted_iota(jnp.int32, (FEATS, points), 0)
    side = (1 - 2 * (me_ref[0] & 1)).astype(F32)
    inner_ref[rhs:, :] = source_rows(rows, x - side, y, z, gain)
    outer_ref[rhs:, :] = source_rows(rows, x + side, y, z, gain)
    own_ref[rhs:, :] = source_rows(rows, x, y, z, gain)
    high, mid, low = parts_of(by_row(rows, (x, y, z, x * x + y * y + z * z, jnp.ones_like(x))))
    target_ref[0:FEATS, :] = high.astype(BF)
    target_ref[FEATS : 2 * FEATS, :] = jnp.where(rows < 10, mid, 0.0).astype(BF)
    target_ref[2 * FEATS : 3 * FEATS, :] = jnp.where(rows < 5, low, 0.0).astype(BF)
    target_ref[3 * FEATS :, :] = jnp.zeros((FEATS, points), BF)
    copies[1].wait()
    all_in = in_ref[...]
    inner_ref[:rhs, :] = all_in
    outer_ref[:rhs, :] = all_in
    own_ref[:rhs, :] = all_in

    for copy in copies[2:]:
        copy.wait()
    blank = jnp.zeros((rhs, leaf), BF)
    lanes = lax.broadcasted_iota(jnp.int32, (rank, 2 * rhs), 1)
    uppers = leaves // BRANCH
    upper = [jnp.zeros((rank, 2 * rhs), F32) for _ in range(uppers)]
    for pair in range(leaves // 2):
        a, b = 2 * pair, 2 * pair + 1
        xa = in_ref[:, a * leaf : (a + 1) * leaf]
        xb = in_ref[:, b * leaf : (b + 1) * leaf]
        weights = jnp.concatenate(
            [jnp.concatenate([xa, blank], axis=1), jnp.concatenate([blank, xb], axis=1)], axis=0
        )
        coef = dot(jnp.concatenate([basis_ref[a], basis_ref[b]], axis=1), weights, NT).astype(BF)
        shard_ref[pair * rank : (pair + 1) * rank, :] = coef
        both = jnp.concatenate(
            [jnp.where(lanes < rhs, coef, jnp.zeros_like(coef)), jnp.where(lanes < rhs, jnp.zeros_like(coef), coef)],
            axis=0,
        )
        moved = jnp.concatenate([transfer_ref[a], transfer_ref[b]], axis=0)
        upper[a // BRANCH] += dot(moved, both, TN)
    for p in range(0, uppers, 2):
        left = upper[p] + pltpu.roll(upper[p], rhs, 1)
        right = upper[p + 1] + pltpu.roll(upper[p + 1], rhs, 1)
        at = leaves // 2 * rank + p // 2 * rank
        shard_ref[at : at + rank, :] = jnp.where(lanes < rhs, left, right).astype(BF)
    at = (leaves + uppers) // 2 * rank
    shard_ref[at:, :] = jnp.zeros((shard_ref.shape[0] - at, 2 * rhs), BF)
    shard_ref[at : at + send_ref.shape[0], 0 : send_ref.shape[1]] = send_ref[...].astype(F32).astype(BF)


def near_kernel(count, first, me_ref, list_ref, own_ref, inner_ref, outer_ref, target_ref, _, out_ref, block_ref):
    wide, points = own_ref.shape
    rhs, some = out_ref.shape
    leaves, near = list_ref.shape
    leaf = points // leaves
    me = me_ref[0]
    start = me * leaves - REACH
    odd = me & 1
    for base, ref in ((2 * (1 - odd) * leaves, inner_ref), (leaves, own_ref), (2 * odd * leaves, outer_ref)):
        for j in range(leaves):
            block_ref[base + j] = ref[:, j * leaf : (j + 1) * leaf]

    def blank(side):
        rows = lax.broadcasted_iota(jnp.int32, (wide - rhs, leaf), 0)
        for j in range(leaves):
            block_ref[side * leaves + j, rhs:, :] = jnp.where(rows == 4, 1.0, 0.0).astype(BF)

    pl.when(me == 0)(lambda: blank(0))
    pl.when(me == count - 1)(lambda: blank(2))

    lanes = lax.broadcasted_iota(jnp.int32, (leaf, 2 * rhs), 1)
    empty = jnp.zeros((4 * FEATS, leaf), BF)
    blank_tile = jnp.zeros((leaf, leaf), BF)
    for l in range(some // leaf):
        rows = target_ref[:, (first + l) * leaf : (first + l + 1) * leaf]
        low = jnp.concatenate([rows, empty], axis=0).T
        high = jnp.concatenate([empty, rows], axis=0).T
        targets = jnp.concatenate(
            [
                jnp.concatenate(two, axis=1)
                for two in ((low, blank_tile), (high, blank_tile), (blank_tile, low), (blank_tile, high))
            ],
            axis=0,
        )
        total = jnp.zeros((leaf, 2 * rhs), F32)
        for k in range(0, near, 8):
            ids = [list_ref[first + l, k + i] - start for i in range(8)]
            feats, values = [], []
            for a, b in zip(ids[0::2], ids[1::2], strict=True):
                feats += [jnp.concatenate([block_ref[a, rhs:, :], block_ref[b, rhs:, :]], axis=1)] * 4
                values.append(jnp.concatenate([block_ref[a, 0:rhs, :], block_ref[b, 0:rhs, :]], axis=1))
            green = lax.rsqrt(dot(targets, jnp.concatenate(feats, axis=0))).astype(BF)
            out = dot(green, jnp.concatenate(values, axis=0), NT)
            total = total + jnp.where(lanes < rhs, out[0:leaf, 0 : 2 * rhs], out[leaf : 2 * leaf, 0 : 2 * rhs])
            total = total + jnp.where(lanes < rhs, out[2 * leaf : 3 * leaf, 2 * rhs :], out[3 * leaf :, 2 * rhs :])
        turned = total.T
        out_ref[:, l * leaf : (l + 1) * leaf] = turned[0:rhs] + turned[rhs:]


def merge_kernel(a_ref, b_ref, _, out_ref):
    deep = a_ref.shape[0]
    out_ref[0:deep] = a_ref[...]
    out_ref[deep:] = b_ref[...]


def coupling_kernel(c_ref, top_ref, out_ref, top_out_ref):
    leaves, far, rank, _ = c_ref.shape
    uppers, top, _, _ = top_ref.shape
    for p in range(uppers):
        for k in range(0, top, 2):
            top_out_ref[p, :, k * rank : (k + 2) * rank] = jnp.concatenate([top_ref[p, k], top_ref[p, k + 1]], axis=1)

    def one(l, carry):
        for k in range(0, far, 2):
            out_ref[l, :, k * rank : (k + 2) * rank] = jnp.concatenate([c_ref[l, k], c_ref[l, k + 1]], axis=1)
        return carry

    lax.fori_loop(0, leaves, one, 0)


def far_kernel(pieces, nears, me_ref, recv_ref, top_ref, *refs):
    piece_refs, refs = refs[:pieces], refs[pieces:]
    near_refs, refs = refs[:nears], refs[nears:]
    coupling_ref, top_coupling_ref, transfer_ref, basis_ref, out_ref, all_ref, owner_vmem, owner_ref, sem = refs
    leaves, rank, leaf = basis_ref.shape
    rhs = out_ref.shape[0]
    far = recv_ref.shape[1]
    uppers, top = top_ref.shape
    me = me_ref[0]
    table_at = (leaves + uppers) // 2 * rank
    table_rows = all_ref.shape[1] - table_at
    rows = lax.broadcasted_iota(jnp.int32, (table_rows, 2 * rhs), 0)
    depth = piece_refs[0].shape[0]
    for j, ref in enumerate(piece_refs):
        for i in range(depth):
            table = ref[i, table_at:, :].astype(F32)
            mine = jnp.sum(jnp.where(rows == me, table, 0.0), axis=0, keepdims=True)
            p = j * depth + i
            owner_vmem[p : p + 1, :] = mine.astype(jnp.int32)
    copy = pltpu.make_async_copy(owner_vmem, owner_ref, sem)
    copy.start()
    for j, ref in enumerate(piece_refs):
        all_ref[j * depth : (j + 1) * depth, :, :] = ref[...]

    lanes = lax.broadcasted_iota(jnp.int32, (rank, 2 * rhs), 1)
    half_of = (lanes >= rhs).astype(jnp.int32)

    def panel(position, index, base):
        at = pl.multiple_of(base + (index >> 1) * rank, rank)
        both = all_ref[position, pl.ds(at, rank), :]
        return jnp.where(half_of == (index & 1), both, jnp.zeros_like(both))

    def sum_of(left, words, base):
        total = jnp.zeros((rank, 2 * rhs), F32)
        for quad in range(0, len(words), 4):
            panels = jnp.concatenate([panel(*word, base) for word in words[quad : quad + 4]], axis=0)
            total = total + dot(left[:, quad * rank : (quad + 4) * rank], panels)
        return total + pltpu.roll(total, rhs, 1)

    moved = []
    for p in range(uppers):
        words = [top_ref[p, k] for k in range(top)]
        field = sum_of(top_coupling_ref[p], [(word >> 8, word & 255) for word in words], leaves // 2 * rank).astype(BF)
        down = transfer_ref[p * BRANCH : (p + 1) * BRANCH].reshape(BRANCH * rank, rank)
        moved.append(dot(down, field))
    copy.wait()

    step = leaves // nears
    for l in range(0, leaves, 2):
        totals = []
        for i in (l, l + 1):
            words = [recv_ref[i, k] for k in range(far)]
            words = [(word >> 8, owner_ref[word >> 8, word & 255]) for word in words]
            at = i % BRANCH * rank
            totals.append(sum_of(coupling_ref[i], words, 0) + moved[i // BRANCH][at : at + rank])
        pair = jnp.where(lanes < rhs, totals[0], totals[1]).T.astype(BF)
        out = dot(pair, jnp.concatenate([basis_ref[l], basis_ref[l + 1]], axis=1))
        for i in range(2):
            j = (l + i) % step
            out_ref[:, (l + i) * leaf : (l + i + 1) * leaf] = (
                near_refs[l // step][:, j * leaf : (j + 1) * leaf]
                + out[i * rhs : (i + 1) * rhs, i * leaf : (i + 1) * leaf]
            )


def body(count, inputs, geometry, leaf_basis, transfer, leaf_coupling, top_coupling, near_list, recv_slot, send_leaf, top_source):
    leaves, leaf, rank = leaf_basis.shape
    rhs = inputs.shape[1]
    points = leaves * leaf
    far = recv_slot.shape[1]
    slots = send_leaf.shape[2]
    uppers = leaves // BRANCH
    me = lax.axis_index("leaf").astype(jnp.int32)
    me_list = me.reshape(1)
    in_t = inputs.T
    basis_t = leaf_basis.transpose(0, 2, 1)
    table_rows = -(-count // 16) * 16
    shard_rows = (leaves + uppers) // 2 * rank + table_rows
    wide = jax.ShapeDtypeStruct((rhs + FEATS, points), BF)
    staged = (in_t, geometry, basis_t, transfer, send_leaf[0])
    shard, to_inner, to_outer, own, targets = pl.pallas_call(
        pack_kernel,
        out_shape=(
            jax.ShapeDtypeStruct((shard_rows, 2 * rhs), BF),
            wide,
            wide,
            wide,
            jax.ShapeDtypeStruct((4 * FEATS, points), BF),
        ),
        in_specs=[SMEM] + [pl.BlockSpec(memory_space=pltpu.HBM)] * 5,
        out_specs=(VMEM,) * 5,
        scratch_shapes=[pltpu.VMEM(a.shape, a.dtype) for a in staged] + [pltpu.SemaphoreType.DMA((5,))],
        compiler_params=params(54),
        cost_estimate=cost(2),
        name="pack",
    )(me_list, *staged)

    def swap(x, bit):
        return lax.ppermute(x, "leaf", [(i, i ^ bit) for i in range(count)])

    base = shard[None]
    high = count // 2
    while high > 8:
        base = jnp.concatenate([base, swap(base, high)], axis=0)
        high //= 2
    deep = base.shape[0]
    far_side = swap(base, 8)
    inner = swap(to_inner, 1)
    outer = lax.ppermute(
        to_outer, "leaf", [pair for i in range(1, count - 1, 2) for pair in ((i, i + 1), (i + 1, i))]
    )
    def place(device):
        gap = lax.bitwise_xor(device, me)
        top = gap >> 4
        out = (gap & 7) * (2 * deep) + ((gap >> 3) & 1) * deep
        bits = deep.bit_length() - 1
        for i in range(bits):
            out = out + ((top >> (bits - 1 - i)) & 1) * (1 << i)
        return out

    recv_words = place(recv_slot // slots) * 256 + recv_slot % slots
    top_words = place(top_source // uppers) * 256 + top_source % uppers

    coupling, top_wide = pl.pallas_call(
        coupling_kernel,
        out_shape=(
            jax.ShapeDtypeStruct((leaves, rank, far * rank), BF),
            jax.ShapeDtypeStruct((uppers, rank, top_source.shape[1] * rank), BF),
        ),
        in_specs=[VMEM, VMEM],
        out_specs=(VMEM,) * 2,
        compiler_params=params(32),
        cost_estimate=cost(0.05),
        name="coupling",
    )(leaf_coupling, top_coupling)

    chunks = 2
    some = leaves // chunks

    def near(c, after):
        return pl.pallas_call(
            functools.partial(near_kernel, count, c * some),
            out_shape=jax.ShapeDtypeStruct((rhs, some * leaf), F32),
            in_specs=[SMEM] * 2 + [VMEM] * 4 + [ANY],
            out_specs=VMEM,
            scratch_shapes=[pltpu.VMEM((leaves + 2 * REACH, rhs + FEATS, leaf), BF)],
            compiler_params=params(32),
            cost_estimate=cost(5),
            name=f"near{c}",
        )(me_list, near_list, own, inner, outer, targets, after)

    def after(x, others):
        return lax.optimization_barrier((x, *others))[0]

    both = pl.pallas_call(
        merge_kernel,
        out_shape=jax.ShapeDtypeStruct((2 * deep, *base.shape[1:]), BF),
        in_specs=[VMEM] * 2 + [ANY],
        out_specs=VMEM,
        compiler_params=params(32),
        cost_estimate=cost(3),
        name="merge",
    )(base, far_side, coupling)
    piece = {0: both}
    piece[4] = swap(both, 4)
    piece[2] = swap(both, 2)
    nears = [near(0, both)]
    piece[4] = after(piece[4], nears)
    piece[6] = swap(piece[4], 2)
    for j in (0, 4, 2):
        piece[j + 1] = swap(piece[j], 1)
    nears += [near(1, piece[4])]
    piece[6] = after(piece[6], nears)
    piece[7] = swap(piece[6], 1)

    out = pl.pallas_call(
        functools.partial(far_kernel, len(piece), chunks),
        out_shape=jax.ShapeDtypeStruct((rhs, points), F32),
        in_specs=[SMEM] * 3 + [VMEM] * (len(piece) + chunks + 4),
        out_specs=VMEM,
        scratch_shapes=[
            pltpu.VMEM((count, shard_rows, 2 * rhs), BF),
            pltpu.VMEM((count, 2 * rhs), jnp.int32),
            pltpu.SMEM((count, 2 * rhs), jnp.int32),
            pltpu.SemaphoreType.DMA,
        ],
        compiler_params=params(48),
        cost_estimate=cost(6),
        name="far",
    )(me_list, recv_words, top_words, *[piece[j] for j in range(len(piece))], *nears, coupling, top_wide, transfer, basis_t)
    return out.T


def solution(mesh):
    spec = ("parts", "leaf")
    in_specs = (
        P(spec, None),
        P(None, spec),
        P(spec, None, None),
        P(spec, None, None),
        P(spec, None, None, None),
        P(spec, None, None, None),
        P(spec, None),
        P(spec, None),
        P(spec, None, None),
        P(spec, None),
    )
    step = functools.partial(body, mesh.shape["leaf"])
    return jax.shard_map(step, mesh=mesh, in_specs=in_specs, out_specs=P(spec, None), check_vma=False)
```

```python
import functools

import jax
import jax.numpy as jnp
from jax import lax
from jax.experimental import pallas as pl
from jax.experimental.pallas import tpu as pltpu
from jax.sharding import PartitionSpec as P

BRANCH = 8
REACH = 16
SCALE = 0.07957747154594767
SOFTEN = 0.0025
BF, F32 = jnp.bfloat16, jnp.float32
NN = (((1,), (0,)), ((), ()))
NT = (((1,), (1,)), ((), ()))
TN = (((0,), (0,)), ((), ()))
VMEM = pl.BlockSpec(memory_space=pltpu.VMEM)
ANY = pl.BlockSpec(memory_space=pl.ANY)
SMEM = pl.BlockSpec(memory_space=pltpu.SMEM)
FEATS = 16


def dot(a, b, dims=NN):
    return lax.dot_general(a, b, dims, preferred_element_type=F32)


def params(mib):
    return pltpu.CompilerParams(vmem_limit_bytes=mib * 2**20)


def cost(us):
    return pl.CostEstimate(flops=int(us * 1e9), bytes_accessed=int(us * 1e6), transcendentals=0)


def parts_of(x):
    high = x.astype(BF).astype(F32)
    mid = (x - high).astype(BF).astype(F32)
    low = (x - high - mid).astype(BF).astype(F32)
    return high, mid, low


def by_row(rows, values):
    which = lax.rem(rows, 5)
    out = jnp.zeros(rows.shape, F32)
    for j, value in enumerate(values):
        out = jnp.where(which == j, value, out)
    return jnp.where(rows < 15, out, 0.0)


def source_rows(rows, x, y, z, gain):
    wide = by_row(
        rows,
        (-2.0 * gain * x, -2.0 * gain * y, -2.0 * gain * z, gain, gain * (x * x + y * y + z * z + SOFTEN)),
    )
    high, mid, low = parts_of(wide)
    return jnp.where(rows < 5, high, jnp.where(rows < 10, mid, low)).astype(BF)


def pack_kernel(me_ref, in_hbm, geo_hbm, basis_hbm, transfer_hbm, send_hbm, shard_ref, inner_ref, first_ref, second_ref, own_ref, target_ref, in_ref, geo_ref, basis_ref, transfer_ref, send_ref, sems):
    pairs = ((geo_hbm, geo_ref), (in_hbm, in_ref), (basis_hbm, basis_ref), (transfer_hbm, transfer_ref), (send_hbm, send_ref))
    copies = [pltpu.make_async_copy(src, dst, sems.at[i]) for i, (src, dst) in enumerate(pairs)]
    for copy in copies:
        copy.start()
    leaves, rank, leaf = basis_ref.shape
    rhs, points = in_ref.shape
    center = (me_ref[0] + 1).astype(F32)
    copies[0].wait()
    x = geo_ref[0:1, :] - center
    y = geo_ref[1:2, :] - 0.5
    z = geo_ref[2:3, :] - 0.5
    scaled = SCALE * geo_ref[3:4, :]
    gain = 1.0 / (scaled * scaled)
    rows = lax.broadcasted_iota(jnp.int32, (FEATS, points), 0)
    side = (1 - 2 * (me_ref[0] & 1)).astype(F32)
    inner_ref[rhs:, :] = source_rows(rows, x - side, y, z, gain)
    odd = (me_ref[0] & 1) == 1
    half = points // 2
    outer = source_rows(rows, x + side, y, z, gain)
    first_ref[rhs:, :] = jnp.where(odd, outer[:, half:], outer[:, :half])
    second_ref[rhs:, :] = jnp.where(odd, outer[:, :half], outer[:, half:])
    own_ref[rhs:, :] = source_rows(rows, x, y, z, gain)
    high, mid, low = parts_of(by_row(rows, (x, y, z, x * x + y * y + z * z, jnp.ones_like(x))))
    target_ref[0:FEATS, :] = high.astype(BF)
    target_ref[FEATS : 2 * FEATS, :] = jnp.where(rows < 10, mid, 0.0).astype(BF)
    target_ref[2 * FEATS : 3 * FEATS, :] = jnp.where(rows < 5, low, 0.0).astype(BF)
    target_ref[3 * FEATS :, :] = jnp.zeros((FEATS, points), BF)
    copies[1].wait()
    all_in = in_ref[...]
    inner_ref[:rhs, :] = all_in
    first_ref[:rhs, :] = jnp.where(odd, all_in[:, half:], all_in[:, :half])
    second_ref[:rhs, :] = jnp.where(odd, all_in[:, :half], all_in[:, half:])
    own_ref[:rhs, :] = all_in

    for copy in copies[2:]:
        copy.wait()
    blank = jnp.zeros((rhs, leaf), BF)
    lanes = lax.broadcasted_iota(jnp.int32, (rank, 2 * rhs), 1)
    uppers = leaves // BRANCH
    upper = [jnp.zeros((rank, 2 * rhs), F32) for _ in range(uppers)]
    for pair in range(leaves // 2):
        a, b = 2 * pair, 2 * pair + 1
        xa = in_ref[:, a * leaf : (a + 1) * leaf]
        xb = in_ref[:, b * leaf : (b + 1) * leaf]
        weights = jnp.concatenate(
            [jnp.concatenate([xa, blank], axis=1), jnp.concatenate([blank, xb], axis=1)], axis=0
        )
        coef = dot(jnp.concatenate([basis_ref[a], basis_ref[b]], axis=1), weights, NT).astype(BF)
        shard_ref[pair * rank : (pair + 1) * rank, :] = coef
        both = jnp.concatenate(
            [jnp.where(lanes < rhs, coef, jnp.zeros_like(coef)), jnp.where(lanes < rhs, jnp.zeros_like(coef), coef)],
            axis=0,
        )
        moved = jnp.concatenate([transfer_ref[a], transfer_ref[b]], axis=0)
        upper[a // BRANCH] += dot(moved, both, TN)
    for p in range(0, uppers, 2):
        left = upper[p] + pltpu.roll(upper[p], rhs, 1)
        right = upper[p + 1] + pltpu.roll(upper[p + 1], rhs, 1)
        at = leaves // 2 * rank + p // 2 * rank
        shard_ref[at : at + rank, :] = jnp.where(lanes < rhs, left, right).astype(BF)
    at = (leaves + uppers) // 2 * rank
    shard_ref[at:, :] = jnp.zeros((shard_ref.shape[0] - at, 2 * rhs), BF)
    shard_ref[at : at + send_ref.shape[0], 0 : send_ref.shape[1]] = send_ref[...].astype(F32).astype(BF)


def near_kernel(count, chunk, me_ref, list_ref, own_ref, inner_ref, *refs):
    outer_refs, (target_ref, _, out_ref, block_ref) = refs[: chunk + 1], refs[chunk + 1 :]
    wide, points = own_ref.shape
    rhs, some = out_ref.shape
    leaves, near = list_ref.shape
    leaf = points // leaves
    me = me_ref[0]
    start = me * leaves - REACH
    odd = me & 1
    first = (leaves // 2) * ((1 - odd) if chunk == 0 else odd)
    half = leaves // 2
    near_half, far_half = half * (1 - odd), half * odd
    fills = [(2 * (1 - odd) * leaves, inner_ref), (leaves, own_ref)]
    fills += [(2 * odd * leaves + at, ref) for at, ref in zip((near_half, far_half), outer_refs)]
    for base, ref in fills:
        for j in range(ref.shape[1] // leaf):
            block_ref[base + j] = ref[:, j * leaf : (j + 1) * leaf]

    def blank(side):
        rows = lax.broadcasted_iota(jnp.int32, (wide - rhs, leaf), 0)
        for j in range(leaves):
            block_ref[side * leaves + j, rhs:, :] = jnp.where(rows == 4, 1.0, 0.0).astype(BF)

    pl.when(me == 0)(lambda: blank(0))
    pl.when(me == count - 1)(lambda: blank(2))

    lanes = lax.broadcasted_iota(jnp.int32, (leaf, 2 * rhs), 1)
    empty = jnp.zeros((4 * FEATS, leaf), BF)
    blank_tile = jnp.zeros((leaf, leaf), BF)
    for l in range(some // leaf):
        rows = target_ref[:, pl.ds(pl.multiple_of((first + l) * leaf, leaf), leaf)]
        low = jnp.concatenate([rows, empty], axis=0).T
        high = jnp.concatenate([empty, rows], axis=0).T
        targets = jnp.concatenate(
            [
                jnp.concatenate(two, axis=1)
                for two in ((low, blank_tile), (high, blank_tile), (blank_tile, low), (blank_tile, high))
            ],
            axis=0,
        )
        total = jnp.zeros((leaf, 2 * rhs), F32)
        for k in range(0, near, 8):
            ids = [list_ref[first + l, k + i] - start for i in range(8)]
            feats, values = [], []
            for a, b in zip(ids[0::2], ids[1::2], strict=True):
                feats += [jnp.concatenate([block_ref[a, rhs:, :], block_ref[b, rhs:, :]], axis=1)] * 4
                values.append(jnp.concatenate([block_ref[a, 0:rhs, :], block_ref[b, 0:rhs, :]], axis=1))
            green = lax.rsqrt(dot(targets, jnp.concatenate(feats, axis=0))).astype(BF)
            out = dot(green, jnp.concatenate(values, axis=0), NT)
            total = total + jnp.where(lanes < rhs, out[0:leaf, 0 : 2 * rhs], out[leaf : 2 * leaf, 0 : 2 * rhs])
            total = total + jnp.where(lanes < rhs, out[2 * leaf : 3 * leaf, 2 * rhs :], out[3 * leaf :, 2 * rhs :])
        turned = total.T
        out_ref[:, l * leaf : (l + 1) * leaf] = turned[0:rhs] + turned[rhs:]


def merge_kernel(a_ref, b_ref, _, out_ref):
    deep = a_ref.shape[0]
    out_ref[0:deep] = a_ref[...]
    out_ref[deep:] = b_ref[...]


def coupling_kernel(c_ref, top_ref, out_ref, top_out_ref):
    leaves, far, rank, _ = c_ref.shape
    uppers, top, _, _ = top_ref.shape
    for p in range(uppers):
        for k in range(0, top, 2):
            top_out_ref[p, :, k * rank : (k + 2) * rank] = jnp.concatenate([top_ref[p, k], top_ref[p, k + 1]], axis=1)

    def one(l, carry):
        for k in range(0, far, 2):
            out_ref[l, :, k * rank : (k + 2) * rank] = jnp.concatenate([c_ref[l, k], c_ref[l, k + 1]], axis=1)
        return carry

    lax.fori_loop(0, leaves, one, 0)


def far_kernel(pieces, nears, me_ref, recv_ref, top_ref, *refs):
    piece_refs, refs = refs[:pieces], refs[pieces:]
    near_refs, refs = refs[:nears], refs[nears:]
    coupling_ref, top_coupling_ref, transfer_ref, basis_ref, out_ref, all_ref, owner_vmem, owner_ref, sem = refs
    leaves, rank, leaf = basis_ref.shape
    rhs = out_ref.shape[0]
    far = recv_ref.shape[1]
    uppers, top = top_ref.shape
    me = me_ref[0]
    table_at = (leaves + uppers) // 2 * rank
    table_rows = all_ref.shape[1] - table_at
    rows = lax.broadcasted_iota(jnp.int32, (table_rows, 2 * rhs), 0)
    depth = piece_refs[0].shape[0]
    for j, ref in enumerate(piece_refs):
        for i in range(depth):
            table = ref[i, table_at:, :].astype(F32)
            mine = jnp.sum(jnp.where(rows == me, table, 0.0), axis=0, keepdims=True)
            p = j * depth + i
            owner_vmem[p : p + 1, :] = mine.astype(jnp.int32)
    copy = pltpu.make_async_copy(owner_vmem, owner_ref, sem)
    copy.start()
    for j, ref in enumerate(piece_refs):
        all_ref[j * depth : (j + 1) * depth, :, :] = ref[...]

    lanes = lax.broadcasted_iota(jnp.int32, (rank, 2 * rhs), 1)
    half_of = (lanes >= rhs).astype(jnp.int32)

    def panel(position, index, base):
        at = pl.multiple_of(base + (index >> 1) * rank, rank)
        both = all_ref[position, pl.ds(at, rank), :]
        return jnp.where(half_of == (index & 1), both, jnp.zeros_like(both))

    def sum_of(left, words, base):
        total = jnp.zeros((rank, 2 * rhs), F32)
        for quad in range(0, len(words), 4):
            panels = jnp.concatenate([panel(*word, base) for word in words[quad : quad + 4]], axis=0)
            total = total + dot(left[:, quad * rank : (quad + 4) * rank], panels)
        return total + pltpu.roll(total, rhs, 1)

    moved = []
    for p in range(uppers):
        words = [top_ref[p, k] for k in range(top)]
        field = sum_of(top_coupling_ref[p], [(word >> 8, word & 255) for word in words], leaves // 2 * rank).astype(BF)
        down = transfer_ref[p * BRANCH : (p + 1) * BRANCH].reshape(BRANCH * rank, rank)
        moved.append(dot(down, field))
    copy.wait()

    step = leaves // nears
    for l in range(0, leaves, 2):
        totals = []
        for i in (l, l + 1):
            words = [recv_ref[i, k] for k in range(far)]
            words = [(word >> 8, owner_ref[word >> 8, word & 255]) for word in words]
            at = i % BRANCH * rank
            totals.append(sum_of(coupling_ref[i], words, 0) + moved[i // BRANCH][at : at + rank])
        pair = jnp.where(lanes < rhs, totals[0], totals[1]).T.astype(BF)
        out = dot(pair, jnp.concatenate([basis_ref[l], basis_ref[l + 1]], axis=1))
        for i in range(2):
            j = (l + i) % step
            columns = slice(j * leaf, (j + 1) * leaf)
            swapped = near_refs[1 - l // step][:, columns]
            near = jnp.where(me & 1 == 1, near_refs[l // step][:, columns], swapped)
            out_ref[:, (l + i) * leaf : (l + i + 1) * leaf] = (
                near + out[i * rhs : (i + 1) * rhs, i * leaf : (i + 1) * leaf]
            )


def body(count, inputs, geometry, leaf_basis, transfer, leaf_coupling, top_coupling, near_list, recv_slot, send_leaf, top_source):
    leaves, leaf, rank = leaf_basis.shape
    rhs = inputs.shape[1]
    points = leaves * leaf
    far = recv_slot.shape[1]
    slots = send_leaf.shape[2]
    uppers = leaves // BRANCH
    me = lax.axis_index("leaf").astype(jnp.int32)
    me_list = me.reshape(1)
    in_t = inputs.T
    basis_t = leaf_basis.transpose(0, 2, 1)
    table_rows = -(-count // 16) * 16
    shard_rows = (leaves + uppers) // 2 * rank + table_rows
    wide = jax.ShapeDtypeStruct((rhs + FEATS, points), BF)
    narrow = jax.ShapeDtypeStruct((rhs + FEATS, points // 2), BF)
    staged = (in_t, geometry, basis_t, transfer, send_leaf[0])
    shard, to_inner, to_first, to_second, own, targets = pl.pallas_call(
        pack_kernel,
        out_shape=(
            jax.ShapeDtypeStruct((shard_rows, 2 * rhs), BF),
            wide,
            narrow,
            narrow,
            wide,
            jax.ShapeDtypeStruct((4 * FEATS, points), BF),
        ),
        in_specs=[SMEM] + [pl.BlockSpec(memory_space=pltpu.HBM)] * 5,
        out_specs=(VMEM,) * 6,
        scratch_shapes=[pltpu.VMEM(a.shape, a.dtype) for a in staged] + [pltpu.SemaphoreType.DMA((5,))],
        compiler_params=params(54),
        cost_estimate=cost(2),
        name="pack",
    )(me_list, *staged)

    def swap(x, bit):
        return lax.ppermute(x, "leaf", [(i, i ^ bit) for i in range(count)])

    base = shard[None]
    high = count // 2
    while high > 8:
        base = jnp.concatenate([base, swap(base, high)], axis=0)
        high //= 2
    deep = base.shape[0]
    far_side = swap(base, 8)
    inner = swap(to_inner, 1)
    outer_pairs = [pair for i in range(1, count - 1, 2) for pair in ((i, i + 1), (i + 1, i))]
    outers = [lax.ppermute(to_first, "leaf", outer_pairs)]
    outers.append(lax.ppermute(to_second, "leaf", outer_pairs))
    def place(device):
        gap = lax.bitwise_xor(device, me)
        top = gap >> 4
        out = (gap & 7) * (2 * deep) + ((gap >> 3) & 1) * deep
        bits = deep.bit_length() - 1
        for i in range(bits):
            out = out + ((top >> (bits - 1 - i)) & 1) * (1 << i)
        return out

    recv_words = place(recv_slot // slots) * 256 + recv_slot % slots
    top_words = place(top_source // uppers) * 256 + top_source % uppers

    coupling, top_wide = pl.pallas_call(
        coupling_kernel,
        out_shape=(
            jax.ShapeDtypeStruct((leaves, rank, far * rank), BF),
            jax.ShapeDtypeStruct((uppers, rank, top_source.shape[1] * rank), BF),
        ),
        in_specs=[VMEM, VMEM],
        out_specs=(VMEM,) * 2,
        compiler_params=params(32),
        cost_estimate=cost(0.05),
        name="coupling",
    )(leaf_coupling, top_coupling)

    chunks = 2
    some = leaves // chunks

    def near(c, after):
        return pl.pallas_call(
            functools.partial(near_kernel, count, c),
            out_shape=jax.ShapeDtypeStruct((rhs, some * leaf), F32),
            in_specs=[SMEM] * 2 + [VMEM] * (4 + c) + [ANY],
            out_specs=VMEM,
            scratch_shapes=[pltpu.VMEM((leaves + 2 * REACH, rhs + FEATS, leaf), BF)],
            compiler_params=params(32),
            cost_estimate=cost(5),
            name=f"near{c}",
        )(me_list, near_list, own, inner, *outers[: c + 1], targets, after)

    def after(x, others):
        return lax.optimization_barrier((x, *others))[0]

    both = pl.pallas_call(
        merge_kernel,
        out_shape=jax.ShapeDtypeStruct((2 * deep, *base.shape[1:]), BF),
        in_specs=[VMEM] * 2 + [ANY],
        out_specs=VMEM,
        compiler_params=params(32),
        cost_estimate=cost(3),
        name="merge",
    )(base, far_side, coupling)
    piece = {0: both}
    piece[4] = swap(both, 4)
    piece[2] = swap(both, 2)
    nears = [near(0, both)]
    piece[4] = after(piece[4], nears)
    piece[6] = swap(piece[4], 2)
    for j in (0, 4, 2):
        piece[j + 1] = swap(piece[j], 1)
    nears += [near(1, piece[4])]
    piece[6] = after(piece[6], nears)
    piece[7] = swap(piece[6], 1)

    out = pl.pallas_call(
        functools.partial(far_kernel, len(piece), chunks),
        out_shape=jax.ShapeDtypeStruct((rhs, points), F32),
        in_specs=[SMEM] * 3 + [VMEM] * (len(piece) + chunks + 4),
        out_specs=VMEM,
        scratch_shapes=[
            pltpu.VMEM((count, shard_rows, 2 * rhs), BF),
            pltpu.VMEM((count, 2 * rhs), jnp.int32),
            pltpu.SMEM((count, 2 * rhs), jnp.int32),
            pltpu.SemaphoreType.DMA,
        ],
        compiler_params=params(48),
        cost_estimate=cost(6),
        name="far",
    )(me_list, recv_words, top_words, *[piece[j] for j in range(len(piece))], *nears, coupling, top_wide, transfer, basis_t)
    return out.T


def solution(mesh):
    spec = ("parts", "leaf")
    in_specs = (
        P(spec, None),
        P(None, spec),
        P(spec, None, None),
        P(spec, None, None),
        P(spec, None, None, None),
        P(spec, None, None, None),
        P(spec, None),
        P(spec, None),
        P(spec, None, None),
        P(spec, None),
    )
    step = functools.partial(body, mesh.shape["leaf"])
    return jax.shard_map(step, mesh=mesh, in_specs=in_specs, out_specs=P(spec, None), check_vma=False)
```

```python
import functools

import jax
import jax.numpy as jnp
from jax import lax
from jax.experimental import pallas as pl
from jax.experimental.pallas import tpu as pltpu
from jax.sharding import PartitionSpec as P

BRANCH = 8
REACH = 16
SCALE = 0.07957747154594767
SOFTEN = 0.0025
BF, F32 = jnp.bfloat16, jnp.float32
NN = (((1,), (0,)), ((), ()))
NT = (((1,), (1,)), ((), ()))
TN = (((0,), (0,)), ((), ()))
VMEM = pl.BlockSpec(memory_space=pltpu.VMEM)
ANY = pl.BlockSpec(memory_space=pl.ANY)
SMEM = pl.BlockSpec(memory_space=pltpu.SMEM)
FEATS = 16


def dot(a, b, dims=NN):
    return lax.dot_general(a, b, dims, preferred_element_type=F32)


def params(mib):
    return pltpu.CompilerParams(vmem_limit_bytes=mib * 2**20)


def cost(us):
    return pl.CostEstimate(flops=int(us * 1e9), bytes_accessed=int(us * 1e6), transcendentals=0)


def parts_of(x):
    high = x.astype(BF).astype(F32)
    mid = (x - high).astype(BF).astype(F32)
    low = (x - high - mid).astype(BF).astype(F32)
    return high, mid, low


def by_row(rows, values):
    which = lax.rem(rows, 5)
    out = jnp.zeros(rows.shape, F32)
    for j, value in enumerate(values):
        out = jnp.where(which == j, value, out)
    return jnp.where(rows < 15, out, 0.0)


def source_rows(rows, x, y, z, gain):
    wide = by_row(
        rows,
        (-2.0 * gain * x, -2.0 * gain * y, -2.0 * gain * z, gain, gain * (x * x + y * y + z * z + SOFTEN)),
    )
    high, mid, low = parts_of(wide)
    return jnp.where(rows < 5, high, jnp.where(rows < 10, mid, low)).astype(BF)


def pack_kernel(me_ref, in_hbm, geo_hbm, basis_hbm, transfer_hbm, send_hbm, shard_ref, inner_ref, first_ref, second_ref, own_ref, target_ref, in_ref, geo_ref, basis_ref, transfer_ref, send_ref, sems):
    pairs = ((geo_hbm, geo_ref), (in_hbm, in_ref), (basis_hbm, basis_ref), (transfer_hbm, transfer_ref), (send_hbm, send_ref))
    copies = [pltpu.make_async_copy(src, dst, sems.at[i]) for i, (src, dst) in enumerate(pairs)]
    for copy in copies:
        copy.start()
    leaves, rank, leaf = basis_ref.shape
    rhs, points = in_ref.shape
    center = (me_ref[0] + 1).astype(F32)
    copies[0].wait()
    x = geo_ref[0:1, :] - center
    y = geo_ref[1:2, :] - 0.5
    z = geo_ref[2:3, :] - 0.5
    scaled = SCALE * geo_ref[3:4, :]
    gain = 1.0 / (scaled * scaled)
    rows = lax.broadcasted_iota(jnp.int32, (FEATS, points), 0)
    side = (1 - 2 * (me_ref[0] & 1)).astype(F32)
    inner_ref[rhs:, :] = source_rows(rows, x - side, y, z, gain)
    odd = (me_ref[0] & 1) == 1
    half = points // 2
    outer = source_rows(rows, x + side, y, z, gain)
    first_ref[rhs:, :] = jnp.where(odd, outer[:, half:], outer[:, :half])
    second_ref[rhs:, :] = jnp.where(odd, outer[:, :half], outer[:, half:])
    own_ref[rhs:, :] = source_rows(rows, x, y, z, gain)
    high, mid, low = parts_of(by_row(rows, (x, y, z, x * x + y * y + z * z, jnp.ones_like(x))))
    target_ref[0:FEATS, :] = high.astype(BF)
    target_ref[FEATS : 2 * FEATS, :] = jnp.where(rows < 10, mid, 0.0).astype(BF)
    target_ref[2 * FEATS : 3 * FEATS, :] = jnp.where(rows < 5, low, 0.0).astype(BF)
    target_ref[3 * FEATS :, :] = jnp.zeros((FEATS, points), BF)
    copies[1].wait()
    all_in = in_ref[...]
    inner_ref[:rhs, :] = all_in
    first_ref[:rhs, :] = jnp.where(odd, all_in[:, half:], all_in[:, :half])
    second_ref[:rhs, :] = jnp.where(odd, all_in[:, :half], all_in[:, half:])
    own_ref[:rhs, :] = all_in

    for copy in copies[2:]:
        copy.wait()
    blank = jnp.zeros((rhs, leaf), BF)
    lanes = lax.broadcasted_iota(jnp.int32, (rank, 2 * rhs), 1)
    uppers = leaves // BRANCH
    upper = [jnp.zeros((rank, 2 * rhs), F32) for _ in range(uppers)]
    for pair in range(leaves // 2):
        a, b = 2 * pair, 2 * pair + 1
        xa = in_ref[:, a * leaf : (a + 1) * leaf]
        xb = in_ref[:, b * leaf : (b + 1) * leaf]
        weights = jnp.concatenate(
            [jnp.concatenate([xa, blank], axis=1), jnp.concatenate([blank, xb], axis=1)], axis=0
        )
        coef = dot(jnp.concatenate([basis_ref[a], basis_ref[b]], axis=1), weights, NT).astype(BF)
        shard_ref[pair * rank : (pair + 1) * rank, :] = coef
        both = jnp.concatenate(
            [jnp.where(lanes < rhs, coef, jnp.zeros_like(coef)), jnp.where(lanes < rhs, jnp.zeros_like(coef), coef)],
            axis=0,
        )
        moved = jnp.concatenate([transfer_ref[a], transfer_ref[b]], axis=0)
        upper[a // BRANCH] += dot(moved, both, TN)
    for p in range(0, uppers, 2):
        left = upper[p] + pltpu.roll(upper[p], rhs, 1)
        right = upper[p + 1] + pltpu.roll(upper[p + 1], rhs, 1)
        at = leaves // 2 * rank + p // 2 * rank
        shard_ref[at : at + rank, :] = jnp.where(lanes < rhs, left, right).astype(BF)
    at = (leaves + uppers) // 2 * rank
    shard_ref[at:, :] = jnp.zeros((shard_ref.shape[0] - at, 2 * rhs), BF)
    shard_ref[at : at + send_ref.shape[0], 0 : send_ref.shape[1]] = send_ref[...].astype(F32).astype(BF)


def near_kernel(count, chunk, me_ref, list_ref, own_ref, inner_ref, *refs):
    outer_refs, (target_ref, _, out_ref, block_ref) = refs[: chunk + 1], refs[chunk + 1 :]
    wide, points = own_ref.shape
    rhs, some = out_ref.shape
    leaves, near = list_ref.shape
    leaf = points // leaves
    me = me_ref[0]
    start = me * leaves - REACH
    odd = me & 1
    first = (leaves // 2) * ((1 - odd) if chunk == 0 else odd)
    half = leaves // 2
    near_half, far_half = half * (1 - odd), half * odd
    fills = [(2 * (1 - odd) * leaves, inner_ref), (leaves, own_ref)]
    fills += [(2 * odd * leaves + at, ref) for at, ref in zip((near_half, far_half), outer_refs)]
    for base, ref in fills:
        for j in range(ref.shape[1] // leaf):
            block_ref[base + j] = ref[:, j * leaf : (j + 1) * leaf]

    def blank(side):
        rows = lax.broadcasted_iota(jnp.int32, (wide - rhs, leaf), 0)
        for j in range(leaves):
            block_ref[side * leaves + j, rhs:, :] = jnp.where(rows == 4, 1.0, 0.0).astype(BF)

    pl.when(me == 0)(lambda: blank(0))
    pl.when(me == count - 1)(lambda: blank(2))

    lanes = lax.broadcasted_iota(jnp.int32, (leaf, 2 * rhs), 1)
    empty = jnp.zeros((4 * FEATS, leaf), BF)
    blank_tile = jnp.zeros((leaf, leaf), BF)
    for l in range(some // leaf):
        rows = target_ref[:, pl.ds(pl.multiple_of((first + l) * leaf, leaf), leaf)]
        low = jnp.concatenate([rows, empty], axis=0).T
        high = jnp.concatenate([empty, rows], axis=0).T
        targets = jnp.concatenate(
            [
                jnp.concatenate(two, axis=1)
                for two in ((low, blank_tile), (high, blank_tile), (blank_tile, low), (blank_tile, high))
            ],
            axis=0,
        )
        total = jnp.zeros((leaf, 2 * rhs), F32)
        for k in range(0, near, 8):
            ids = [list_ref[first + l, k + i] - start for i in range(8)]
            feats, values = [], []
            for a, b in zip(ids[0::2], ids[1::2], strict=True):
                feats += [jnp.concatenate([block_ref[a, rhs:, :], block_ref[b, rhs:, :]], axis=1)] * 4
                values.append(jnp.concatenate([block_ref[a, 0:rhs, :], block_ref[b, 0:rhs, :]], axis=1))
            green = lax.rsqrt(dot(targets, jnp.concatenate(feats, axis=0))).astype(BF)
            out = dot(green, jnp.concatenate(values, axis=0), NT)
            total = total + jnp.where(lanes < rhs, out[0:leaf, 0 : 2 * rhs], out[leaf : 2 * leaf, 0 : 2 * rhs])
            total = total + jnp.where(lanes < rhs, out[2 * leaf : 3 * leaf, 2 * rhs :], out[3 * leaf :, 2 * rhs :])
        turned = total.T
        out_ref[:, l * leaf : (l + 1) * leaf] = turned[0:rhs] + turned[rhs:]


def merge_kernel(a_ref, b_ref, out_ref):
    deep = a_ref.shape[0]
    out_ref[0:deep] = a_ref[...]
    out_ref[deep:] = b_ref[...]


def coupling_kernel(_, c_ref, top_ref, out_ref, top_out_ref):
    leaves, far, rank, _ = c_ref.shape
    uppers, top, _, _ = top_ref.shape
    for p in range(uppers):
        for k in range(0, top, 2):
            top_out_ref[p, :, k * rank : (k + 2) * rank] = jnp.concatenate([top_ref[p, k], top_ref[p, k + 1]], axis=1)

    def one(l, carry):
        for k in range(0, far, 2):
            out_ref[l, :, k * rank : (k + 2) * rank] = jnp.concatenate([c_ref[l, k], c_ref[l, k + 1]], axis=1)
        return carry

    lax.fori_loop(0, leaves, one, 0)


def far_kernel(pieces, nears, me_ref, recv_ref, top_ref, *refs):
    piece_refs, refs = refs[:pieces], refs[pieces:]
    near_refs, refs = refs[:nears], refs[nears:]
    coupling_ref, top_coupling_ref, transfer_ref, basis_ref, out_ref, all_ref, owner_vmem, owner_ref, sem = refs
    leaves, rank, leaf = basis_ref.shape
    rhs = out_ref.shape[0]
    far = recv_ref.shape[1]
    uppers, top = top_ref.shape
    me = me_ref[0]
    table_at = (leaves + uppers) // 2 * rank
    table_rows = all_ref.shape[1] - table_at
    rows = lax.broadcasted_iota(jnp.int32, (table_rows, 2 * rhs), 0)
    depth = piece_refs[0].shape[0]
    for j, ref in enumerate(piece_refs):
        for i in range(depth):
            table = ref[i, table_at:, :].astype(F32)
            mine = jnp.sum(jnp.where(rows == me, table, 0.0), axis=0, keepdims=True)
            p = j * depth + i
            owner_vmem[p : p + 1, :] = mine.astype(jnp.int32)
    copy = pltpu.make_async_copy(owner_vmem, owner_ref, sem)
    copy.start()
    for j, ref in enumerate(piece_refs):
        all_ref[j * depth : (j + 1) * depth, :, :] = ref[...]

    lanes = lax.broadcasted_iota(jnp.int32, (rank, 2 * rhs), 1)
    half_of = (lanes >= rhs).astype(jnp.int32)

    def panel(position, index, base):
        at = pl.multiple_of(base + (index >> 1) * rank, rank)
        both = all_ref[position, pl.ds(at, rank), :]
        return jnp.where(half_of == (index & 1), both, jnp.zeros_like(both))

    def sum_of(left, words, base):
        total = jnp.zeros((rank, 2 * rhs), F32)
        for quad in range(0, len(words), 4):
            panels = jnp.concatenate([panel(*word, base) for word in words[quad : quad + 4]], axis=0)
            total = total + dot(left[:, quad * rank : (quad + 4) * rank], panels)
        return total + pltpu.roll(total, rhs, 1)

    moved = []
    for p in range(uppers):
        words = [top_ref[p, k] for k in range(top)]
        field = sum_of(top_coupling_ref[p], [(word >> 8, word & 255) for word in words], leaves // 2 * rank).astype(BF)
        down = transfer_ref[p * BRANCH : (p + 1) * BRANCH].reshape(BRANCH * rank, rank)
        moved.append(dot(down, field))
    copy.wait()

    step = leaves // nears
    for l in range(0, leaves, 2):
        totals = []
        for i in (l, l + 1):
            words = [recv_ref[i, k] for k in range(far)]
            words = [(word >> 8, owner_ref[word >> 8, word & 255]) for word in words]
            at = i % BRANCH * rank
            totals.append(sum_of(coupling_ref[i], words, 0) + moved[i // BRANCH][at : at + rank])
        pair = jnp.where(lanes < rhs, totals[0], totals[1]).T.astype(BF)
        out = dot(pair, jnp.concatenate([basis_ref[l], basis_ref[l + 1]], axis=1))
        for i in range(2):
            j = (l + i) % step
            columns = slice(j * leaf, (j + 1) * leaf)
            swapped = near_refs[1 - l // step][:, columns]
            near = jnp.where(me & 1 == 1, near_refs[l // step][:, columns], swapped)
            out_ref[:, (l + i) * leaf : (l + i + 1) * leaf] = (
                near + out[i * rhs : (i + 1) * rhs, i * leaf : (i + 1) * leaf]
            )


def body(count, inputs, geometry, leaf_basis, transfer, leaf_coupling, top_coupling, near_list, recv_slot, send_leaf, top_source):
    leaves, leaf, rank = leaf_basis.shape
    rhs = inputs.shape[1]
    points = leaves * leaf
    far = recv_slot.shape[1]
    slots = send_leaf.shape[2]
    uppers = leaves // BRANCH
    me = lax.axis_index("leaf").astype(jnp.int32)
    me_list = me.reshape(1)
    in_t = inputs.T
    basis_t = leaf_basis.transpose(0, 2, 1)
    table_rows = -(-count // 16) * 16
    shard_rows = (leaves + uppers) // 2 * rank + table_rows
    wide = jax.ShapeDtypeStruct((rhs + FEATS, points), BF)
    narrow = jax.ShapeDtypeStruct((rhs + FEATS, points // 2), BF)
    staged = (in_t, geometry, basis_t, transfer, send_leaf[0])
    shard, to_inner, to_first, to_second, own, targets = pl.pallas_call(
        pack_kernel,
        out_shape=(
            jax.ShapeDtypeStruct((shard_rows, 2 * rhs), BF),
            wide,
            narrow,
            narrow,
            wide,
            jax.ShapeDtypeStruct((4 * FEATS, points), BF),
        ),
        in_specs=[SMEM] + [pl.BlockSpec(memory_space=pltpu.HBM)] * 5,
        out_specs=(VMEM,) * 6,
        scratch_shapes=[pltpu.VMEM(a.shape, a.dtype) for a in staged] + [pltpu.SemaphoreType.DMA((5,))],
        compiler_params=params(54),
        cost_estimate=cost(2),
        name="pack",
    )(me_list, *staged)

    def swap(x, bit):
        return lax.ppermute(x, "leaf", [(i, i ^ bit) for i in range(count)])

    base = shard[None]
    high = count // 2
    while high > 8:
        base = jnp.concatenate([base, swap(base, high)], axis=0)
        high //= 2
    deep = base.shape[0]
    far_side = swap(base, 8)
    inner = swap(to_inner, 1)
    outer_pairs = [pair for i in range(1, count - 1, 2) for pair in ((i, i + 1), (i + 1, i))]
    outers = [lax.ppermute(to_first, "leaf", outer_pairs)]
    outers.append(lax.ppermute(to_second, "leaf", outer_pairs))
    def place(device):
        gap = lax.bitwise_xor(device, me)
        top = gap >> 4
        out = (gap & 7) * (2 * deep) + ((gap >> 3) & 1) * deep
        bits = deep.bit_length() - 1
        for i in range(bits):
            out = out + ((top >> (bits - 1 - i)) & 1) * (1 << i)
        return out

    recv_words = place(recv_slot // slots) * 256 + recv_slot % slots
    top_words = place(top_source // uppers) * 256 + top_source % uppers

    chunks = 2
    some = leaves // chunks

    def near(c, after):
        return pl.pallas_call(
            functools.partial(near_kernel, count, c),
            out_shape=jax.ShapeDtypeStruct((rhs, some * leaf), F32),
            in_specs=[SMEM] * 2 + [VMEM] * (4 + c) + [ANY],
            out_specs=VMEM,
            scratch_shapes=[pltpu.VMEM((leaves + 2 * REACH, rhs + FEATS, leaf), BF)],
            compiler_params=params(32),
            cost_estimate=cost(5),
            name=f"near{c}",
        )(me_list, near_list, own, inner, *outers[: c + 1], targets, after)

    def after(x, others):
        return lax.optimization_barrier((x, *others))[0]

    both = pl.pallas_call(
        merge_kernel,
        out_shape=jax.ShapeDtypeStruct((2 * deep, *base.shape[1:]), BF),
        in_specs=[VMEM] * 2,
        out_specs=VMEM,
        compiler_params=params(32),
        cost_estimate=cost(3),
        name="merge",
    )(base, far_side)
    piece = {0: both}
    piece[4] = swap(both, 4)
    piece[2] = swap(both, 2)
    nears = [near(0, both)]
    piece[4] = after(piece[4], nears)
    piece[6] = swap(piece[4], 2)
    for j in (0, 4, 2):
        piece[j + 1] = swap(piece[j], 1)
    nears += [near(1, piece[4])]
    coupling, top_wide = pl.pallas_call(
        coupling_kernel,
        out_shape=(
            jax.ShapeDtypeStruct((leaves, rank, far * rank), BF),
            jax.ShapeDtypeStruct((uppers, rank, top_source.shape[1] * rank), BF),
        ),
        in_specs=[ANY, VMEM, VMEM],
        out_specs=(VMEM,) * 2,
        compiler_params=params(32),
        cost_estimate=cost(0.05),
        name="coupling",
    )(nears[1], leaf_coupling, top_coupling)
    piece[6] = after(piece[6], [*nears, coupling])
    piece[7] = swap(piece[6], 1)

    out = pl.pallas_call(
        functools.partial(far_kernel, len(piece), chunks),
        out_shape=jax.ShapeDtypeStruct((rhs, points), F32),
        in_specs=[SMEM] * 3 + [VMEM] * (len(piece) + chunks + 4),
        out_specs=VMEM,
        scratch_shapes=[
            pltpu.VMEM((count, shard_rows, 2 * rhs), BF),
            pltpu.VMEM((count, 2 * rhs), jnp.int32),
            pltpu.SMEM((count, 2 * rhs), jnp.int32),
            pltpu.SemaphoreType.DMA,
        ],
        compiler_params=params(48),
        cost_estimate=cost(6),
        name="far",
    )(me_list, recv_words, top_words, *[piece[j] for j in range(len(piece))], *nears, coupling, top_wide, transfer, basis_t)
    return out.T


def solution(mesh):
    spec = ("parts", "leaf")
    in_specs = (
        P(spec, None),
        P(None, spec),
        P(spec, None, None),
        P(spec, None, None),
        P(spec, None, None, None),
        P(spec, None, None, None),
        P(spec, None),
        P(spec, None),
        P(spec, None, None),
        P(spec, None),
    )
    step = functools.partial(body, mesh.shape["leaf"])
    return jax.shard_map(step, mesh=mesh, in_specs=in_specs, out_specs=P(spec, None), check_vma=False)
```
